512 devices in a mesh: rows: 8 (over x, y_lo), cols: 64 (over y_hi, z, core).
Axes of the slice: x: 4, y: 4 (y_hi: 2, y_lo: 2; y = y_hi * 2 + y_lo), z: 16, core: 2. Of those that a mesh axis runs over, the one named last changes fastest.
Arguments:
- grad_out: bfloat16 [1024, 6144], P('cols', 'rows'), may hold values from -6 to 6
- ctx_code: bfloat16 [1024, 6144], P('rows', 'cols'), may hold values from -3 to 3
- ctx_scale: float32 [1024, 192], P('rows', 'cols'), may hold values from 0.5 to 2
- stream_code: bfloat16 [1024, 6144], P('cols', 'rows'), may hold values from -3 to 3
- stream_scale: float32 [1024, 192], P('cols', 'rows'), may hold values from 0.5 to 2
- hidden_code: bfloat16 [1024, 24576], P('rows', 'cols'), may hold values from -3 to 3
- hidden_scale: float32 [1024, 768], P('rows', 'cols'), may hold values from 0.5 to 2
- out_weight: bfloat16 [6144, 6144], P('cols', 'rows'), may hold values from -0.078125 to 0.078125
- up_weight: bfloat16 [6144, 24576], P('rows', 'cols'), may hold values from -0.078125 to 0.078125
- down_weight: bfloat16 [24576, 6144], P('cols', 'rows'), may hold values from -0.0390625 to 0.0390625
Outputs:
- grad_ctx: bfloat16 [1024, 6144], P('rows', 'cols')
- grad_out_weight: float32 [6144, 6144], P('cols', 'rows')
- grad_up_weight: float32 [6144, 24576], P('rows', 'cols')
- grad_down_weight: float32 [24576, 6144], P('cols', 'rows')
The draws below stay inside these ranges and needn't reach their ends.
All inputs are finite; a program needn't handle non-finite values.
Results may differ from the reference program's by a relative error of at most 0.034.
Values may be sent and summed in bfloat16 or wider, within the bound.
No kernel may reach another device: no remote copies, remote signals or barrier semaphores. Data moves between devices by JAX's collectives and lax.ppermute only.
A program may use at most 64 MiB of HBM per device.

```python
import math
import jax
import jax.numpy as jnp
from jax import lax

D = 6144
FF = 24576
QBLOCK = 32
TOKENS = 1024
N_ROWS = 8


def level_of(key, dims, split, smallest, high):
    def one(dim, shards_of):
        draws = jax.random.uniform(jax.random.fold_in(jax.random.fold_in(key, 6), dim), (shards_of,), jnp.float32, smallest / len(split), high / len(split))
        return jnp.repeat(jnp.exp(draws), dims[dim] // shards_of).reshape((-1,) + (1,) * (len(dims) - dim - 1))

    factor_of = one(*split[0])
    for cut in split[1:]:
        factor_of = factor_of * one(*cut)
    return factor_of


def noise(stream_key, dims, spread, bound, shards=(), held_as=jnp.bfloat16):
    values = jax.random.normal(stream_key, dims, jnp.float32) * spread
    if len(shards) > 0:
        values = level_of(stream_key, dims, shards, -0.22, 0.18) * values
    return jnp.clip(values, min=-bound, max=bound).astype(held_as)


def setup_inputs(seed: int = 0) -> dict:
    key_list = jax.random.split(jax.random.key(seed), 11)
    return {
        "grad_out": noise(key_list[0], (TOKENS, D), 1.0, 6.0, ((0, 64), (1, 8))),
        "ctx_code": noise(key_list[1], (TOKENS, D), 0.5, 3.0, ((0, 8), (1, 64))),
        "ctx_scale": jnp.clip(jnp.exp(math.log(2.0) - 1.3862944 * jax.random.uniform(key_list[2], (TOKENS, D // QBLOCK), jnp.float32) ** level_of(key_list[2], (TOKENS, D // QBLOCK), ((0, 8), (1, 64)), -0.2, 0.2)), 0.5, 2.0),
        "stream_code": noise(key_list[3], (TOKENS, D), 0.5, 3.0, ((0, 64), (1, 8))),
        "stream_scale": jnp.clip(jnp.exp(math.log(2.0) - 1.3862944 * jax.random.uniform(key_list[4], (TOKENS, D // QBLOCK), jnp.float32) ** level_of(key_list[4], (TOKENS, D // QBLOCK), ((0, 64), (1, 8)), -0.2, 0.2)), 0.5, 2.0),
        "hidden_code": noise(key_list[5], (TOKENS, FF), 0.5, 3.0, ((0, 8), (1, 64))),
        "hidden_scale": jnp.clip(jnp.exp(math.log(2.0) - 1.3862944 * jax.random.uniform(key_list[6], (TOKENS, FF // QBLOCK), jnp.float32) ** level_of(key_list[6], (TOKENS, FF // QBLOCK), ((0, 8), (1, 64)), -0.2, 0.2)), 0.5, 2.0),
        "out_weight": noise(key_list[7], (D, D), D ** -0.5, 0.078125, ((0, 64), (1, 8))),
        "up_weight": noise(key_list[8], (D, FF), D ** -0.5, 0.078125, ((0, 8), (1, 64))),
        "down_weight": noise(key_list[9], (FF, D), FF ** -0.5, 0.0390625, ((0, 64), (1, 8))),
    }


def restore(code, scale):
    count, width = code.shape
    blocks = code.astype(jnp.float32).reshape(count, width // QBLOCK, QBLOCK) * scale[:, :, None]
    return blocks.reshape(count, width).astype(jnp.bfloat16)


def blocked_product(left, right):
    span = D // N_ROWS
    total = jnp.zeros((left.shape[0], right.shape[0]), jnp.float32)
    for block in range(N_ROWS):
        partial_term = jnp.dot(left[:, block * span:(block + 1) * span], right[:, block * span:(block + 1) * span].T, preferred_element_type=jnp.float32)
        rounded = lax.optimization_barrier(partial_term.astype(jnp.bfloat16))
        total = total + rounded.astype(jnp.float32)
    return total


def reference(grad_out, ctx_code, ctx_scale, stream_code, stream_scale, hidden_code, hidden_scale, out_weight, up_weight, down_weight):
    context = restore(ctx_code, ctx_scale)
    stream = restore(stream_code, stream_scale)
    preact = restore(hidden_code, hidden_scale).astype(jnp.float32)
    grad_act = blocked_product(grad_out, down_weight)
    positive = jnp.maximum(preact, 0.0)
    grad_pre = (grad_act * 2.0 * positive).astype(jnp.bfloat16)
    act = (positive * positive).astype(jnp.bfloat16)
    grad_down = jnp.dot(act.T, grad_out, preferred_element_type=jnp.float32)
    grad_up = jnp.dot(stream.T, grad_pre, preferred_element_type=jnp.float32)
    grad_stream = (grad_out.astype(jnp.float32) + jnp.dot(grad_pre, up_weight.T, preferred_element_type=jnp.float32)).astype(jnp.bfloat16)
    grad_outw = jnp.dot(context.T, grad_stream, preferred_element_type=jnp.float32)
    grad_ctx = blocked_product(grad_stream, out_weight).astype(jnp.bfloat16)
    return grad_ctx, grad_outw, grad_up, grad_down
```

```python
import jax
import jax.numpy as jnp
from jax import lax
from jax.sharding import Mesh
from jax.sharding import PartitionSpec as P

QBLOCK = 32
ROWS = ("x", "yl")
COLS = ("yh", "z", "c")
SWAP = ((0, 1), (1, 0))


def restore(code, scale):
    count, width = code.shape
    blocks = code.astype(jnp.float32).reshape(count, width // QBLOCK, QBLOCK) * scale[:, :, None]
    return blocks.reshape(count, width).astype(jnp.bfloat16)


def dot_nt(left, right):
    return lax.dot_general(
        left, right, (((1,), (1,)), ((), ())), preferred_element_type=jnp.float32
    )


def dot_tn(left, right):
    return lax.dot_general(
        left, right, (((0,), (0,)), ((), ())), preferred_element_type=jnp.float32
    )


def local(
    grad_out,
    ctx_code,
    ctx_scale,
    stream_code,
    stream_scale,
    hidden_code,
    hidden_scale,
    out_weight,
    up_weight,
    down_weight,
):
    core = lax.axis_index("c")
    half = lax.axis_index("yh")
    n_rows, n_z = lax.axis_size(ROWS), lax.axis_size("z")
    per = grad_out.shape[0]
    runs = n_z * 2 // n_rows
    features = grad_out.shape[1]

    def own_first(block):
        width = block.shape[1]
        parts = block.reshape(runs, 2, per, width)
        one, two = parts[:, 0], parts[:, 1]
        first = jnp.where(core == 0, one, two)
        second = jnp.where(core == 0, two, one)
        return jnp.stack([first, second]).reshape(block.shape)

    def natural(block):
        width = block.shape[1]
        parts = block.reshape(2, runs, per, width)
        one = jnp.where(core == 0, parts[0], parts[1])
        two = jnp.where(core == 0, parts[1], parts[0])
        return jnp.stack([one, two], axis=1).reshape(block.shape)

    def swap(block, axis):
        return lax.ppermute(block, axis, SWAP)

    def scatter_rows(own, other):
        width = own.shape[1]
        sent = jnp.stack(
            [own.reshape(n_rows, -1, width), other.reshape(n_rows, -1, width)], axis=1
        )
        came = lax.all_to_all(sent, ROWS, 0, 0, tiled=True)
        return jnp.sum(came.astype(jnp.float32), axis=0).reshape(-1, width)

    def gather_z(pair):
        return lax.all_gather(pair, "z", axis=1).reshape(-1, features)

    stream = restore(stream_code, stream_scale)
    positive = jnp.maximum(
        own_first(restore(hidden_code, hidden_scale)).astype(jnp.float32), 0.0
    )
    act = (positive * positive).astype(jnp.bfloat16)
    context = own_first(restore(ctx_code, ctx_scale))
    hidden_width, ctx_width = act.shape[1], context.shape[1]
    padding = jnp.zeros((act.shape[0], 512 - hidden_width - ctx_width), jnp.bfloat16)
    saved = jnp.concatenate([act, context, padding], axis=1)
    saved_all = lax.all_gather(saved, ROWS, axis=0)

    both = lax.all_gather(jnp.stack([grad_out, stream]), "yh", axis=0)
    stream_all = lax.all_gather(both[:, 1], ("z", "c"), axis=0)
    grad_own = gather_z(both[:, 0])
    grad_other = swap(grad_own, "c")

    grad_act = scatter_rows(
        dot_nt(grad_own, down_weight).astype(jnp.bfloat16),
        dot_nt(grad_other, down_weight).astype(jnp.bfloat16),
    )
    grad_pre = (grad_act * 2.0 * positive).astype(jnp.bfloat16)
    copies = lax.optimization_barrier(
        jnp.broadcast_to(grad_pre[None], (n_rows,) + grad_pre.shape)
    )
    grad_pre_all = lax.all_to_all(copies, ROWS, 0, 0, tiled=True).reshape(
        n_rows, 2, -1, hidden_width
    )
    pre_own = grad_pre_all[:, 0].reshape(-1, hidden_width)
    pre_other = grad_pre_all[:, 1].reshape(-1, hidden_width)

    came = swap(dot_nt(pre_other, up_weight).astype(jnp.bfloat16), "c")
    part = (dot_nt(pre_own, up_weight) + came.astype(jnp.float32)).reshape(2, -1, features)
    keep = lax.dynamic_index_in_dim(part, half, 0, keepdims=False)
    send = lax.dynamic_index_in_dim(part, 1 - half, 0, keepdims=False).astype(jnp.bfloat16)
    part = (keep + swap(send, "yh").astype(jnp.float32)).astype(jnp.bfloat16)
    came = lax.all_to_all(part.reshape(n_z, per, features), "z", 0, 0, tiled=True)
    summed = jnp.sum(came.astype(jnp.float32), axis=0)
    grad_stream = (grad_out.astype(jnp.float32) + summed).astype(jnp.bfloat16)

    gs_own = gather_z(lax.all_gather(grad_stream, "yh", axis=0))
    gs_other = swap(gs_own, "c")
    grad_ctx = natural(
        scatter_rows(
            dot_nt(gs_own, out_weight).astype(jnp.bfloat16),
            dot_nt(gs_other, out_weight).astype(jnp.bfloat16),
        )
    ).astype(jnp.bfloat16)

    saved_own = saved_all.reshape(n_rows, 2, -1, 512)[:, 0].reshape(-1, 512)
    saved_other = saved_all.reshape(n_rows, 2, -1, 512)[:, 1].reshape(-1, 512)
    act_own, act_other = saved_own[:, :hidden_width], saved_other[:, :hidden_width]
    ctx_own = saved_own[:, hidden_width : hidden_width + ctx_width]
    ctx_other = saved_other[:, hidden_width : hidden_width + ctx_width]
    by_core = stream_all.reshape(n_z, 2, 2, per, features)
    stream_own = lax.dynamic_index_in_dim(by_core, core, 1, keepdims=False)
    stream_other = lax.dynamic_index_in_dim(by_core, 1 - core, 1, keepdims=False)
    stream_own = jnp.swapaxes(stream_own, 0, 1).reshape(-1, features)
    stream_other = jnp.swapaxes(stream_other, 0, 1).reshape(-1, features)

    grad_down = dot_tn(act_own, grad_own) + dot_tn(act_other, grad_other)
    grad_up = dot_tn(stream_own, pre_own) + dot_tn(stream_other, pre_other)
    grad_outw = dot_tn(ctx_own, gs_own) + dot_tn(ctx_other, gs_other)
    return (grad_ctx, grad_outw, grad_up, grad_down)


def solution(mesh):
    parts = Mesh(mesh.devices.reshape(4, 2, 2, 16, 2), ROWS + COLS)
    by_cols, by_rows = P(COLS, ROWS), P(ROWS, COLS)
    in_specs = (
        by_cols,
        by_rows,
        by_rows,
        by_cols,
        by_cols,
        by_rows,
        by_rows,
        by_cols,
        by_rows,
        by_cols,
    )
    out_specs = (by_rows, by_cols, by_rows, by_cols)
    return jax.shard_map(local, mesh=parts, in_specs=in_specs, out_specs=out_specs, check_vma=False)
```

```python
import jax
import jax.numpy as jnp
from jax import lax
from jax.sharding import Mesh
from jax.sharding import PartitionSpec as P

QBLOCK = 32
ROWS = ("x", "yl")
COLS = ("yh", "z", "c")
SWAP = ((0, 1), (1, 0))


def restore(code, scale):
    count, width = code.shape
    blocks = code.astype(jnp.float32).reshape(count, width // QBLOCK, QBLOCK) * scale[:, :, None]
    return blocks.reshape(count, width).astype(jnp.bfloat16)


def dot_nt(left, right):
    return lax.dot_general(
        left, right, (((1,), (1,)), ((), ())), preferred_element_type=jnp.float32
    )


def dot_tn(left, right):
    return lax.dot_general(
        left, right, (((0,), (0,)), ((), ())), preferred_element_type=jnp.float32
    )


def local(
    grad_out,
    ctx_code,
    ctx_scale,
    stream_code,
    stream_scale,
    hidden_code,
    hidden_scale,
    out_weight,
    up_weight,
    down_weight,
):
    core = lax.axis_index("c")
    n_rows, n_z = lax.axis_size(ROWS), lax.axis_size("z")
    per = grad_out.shape[0]
    runs = n_z * 2 // n_rows
    features = grad_out.shape[1]

    def own_first(block):
        width = block.shape[1]
        parts = block.reshape(runs, 2, per, width)
        one, two = parts[:, 0], parts[:, 1]
        first = jnp.where(core == 0, one, two)
        second = jnp.where(core == 0, two, one)
        return jnp.stack([first, second]).reshape(block.shape)

    def natural(block):
        width = block.shape[1]
        parts = block.reshape(2, runs, per, width)
        one = jnp.where(core == 0, parts[0], parts[1])
        two = jnp.where(core == 0, parts[1], parts[0])
        return jnp.stack([one, two], axis=1).reshape(block.shape)

    def swap(block, axis):
        return lax.ppermute(block, axis, SWAP)

    def scatter_rows(own, other):
        width = own.shape[1]
        sent = jnp.stack([by_row(own), by_row(other)], axis=1)
        came = lax.all_to_all(sent, ROWS, 0, 0, tiled=True)
        return jnp.sum(came.astype(jnp.float32), axis=0).reshape(-1, width)

    def by_row(block):
        width = block.shape[1]
        parts = block.reshape(n_rows // 2, runs, 2, per, width)
        return parts.transpose(2, 0, 1, 3, 4).reshape(n_rows, runs * per, width)

    def by_z(block):
        width = block.shape[-1]
        parts = block.reshape(2, n_z, per, width)
        return jnp.swapaxes(parts, 0, 1).reshape(-1, width)

    def gather_z(pair):
        return lax.all_gather(pair.reshape(-1, features), "z", axis=0, tiled=True)

    def gather_rows(block):
        copies = lax.optimization_barrier(
            jnp.broadcast_to(block[None], (n_rows,) + block.shape)
        )
        every = lax.all_to_all(copies, ROWS, 0, 0, tiled=True)
        return every.reshape(n_rows, 2, -1, block.shape[1])

    stream = restore(stream_code, stream_scale)
    positive = jnp.maximum(
        own_first(restore(hidden_code, hidden_scale)).astype(jnp.float32), 0.0
    )
    act = (positive * positive).astype(jnp.bfloat16)
    context = own_first(restore(ctx_code, ctx_scale))
    hidden_width = act.shape[1]
    saved = jnp.concatenate([act, context], axis=1)

    both = lax.all_gather(jnp.stack([grad_out, stream]), "yh", axis=0)
    stream_all = lax.all_gather(both[:, 1], ("z", "c"), axis=0)
    grad_own = gather_z(both[:, 0])
    grad_other = swap(grad_own, "c")

    grad_act = scatter_rows(
        dot_nt(grad_own, down_weight).astype(jnp.bfloat16),
        dot_nt(grad_other, down_weight).astype(jnp.bfloat16),
    )
    grad_pre = (grad_act * 2.0 * positive).astype(jnp.bfloat16)
    grad_pre_all = gather_rows(grad_pre)
    pre_own = by_z(grad_pre_all[:, 0])
    pre_other = by_z(grad_pre_all[:, 1])

    came = swap(dot_nt(pre_other, up_weight).astype(jnp.bfloat16), "c")
    part = (dot_nt(pre_own, up_weight) + came.astype(jnp.float32)).astype(jnp.bfloat16)
    part, saved = lax.optimization_barrier((part, saved))
    saved_all = lax.all_gather(saved, ROWS, axis=0)
    came = lax.all_to_all(part.reshape(n_z, 2 * per, features), "z", 0, 0, tiled=True)
    came, saved_all = lax.optimization_barrier((came, saved_all))
    part = jnp.sum(came.astype(jnp.float32), axis=0).astype(jnp.bfloat16)
    summed = part.astype(jnp.float32) + swap(part, "yh").astype(jnp.float32)
    pair_out = both[:, 0].reshape(2 * per, features).astype(jnp.float32)
    grad_stream = (pair_out + summed).astype(jnp.bfloat16)

    gs_own = gather_z(grad_stream)
    stream_all, gs_late = lax.optimization_barrier((stream_all, gs_own))
    gs_other = swap(gs_own, "c")
    grad_ctx = natural(
        scatter_rows(
            dot_nt(gs_own, out_weight).astype(jnp.bfloat16),
            dot_nt(gs_other, out_weight).astype(jnp.bfloat16),
        )
    ).astype(jnp.bfloat16)

    saved_pairs = saved_all.reshape(n_rows, 2, -1, saved_all.shape[-1])
    saved_own, saved_other = by_z(saved_pairs[:, 0]), by_z(saved_pairs[:, 1])
    act_own, act_other = saved_own[:, :hidden_width], saved_other[:, :hidden_width]
    ctx_own = saved_own[:, hidden_width:]
    ctx_other = saved_other[:, hidden_width:]
    by_core = stream_all.reshape(n_z, 2, 2 * per, features)
    stream_own = lax.dynamic_index_in_dim(by_core, core, 1, keepdims=False)
    stream_other = lax.dynamic_index_in_dim(by_core, 1 - core, 1, keepdims=False)
    stream_own = stream_own.reshape(-1, features)
    stream_other = stream_other.reshape(-1, features)

    grad_down = dot_tn(act_own, grad_own) + dot_tn(act_other, grad_other)
    grad_up = dot_tn(stream_own, pre_own) + dot_tn(stream_other, pre_other)
    grad_outw = dot_tn(ctx_own, gs_late) + dot_tn(ctx_other, gs_other)
    return (grad_ctx, grad_outw, grad_up, grad_down)


def solution(mesh):
    parts = Mesh(mesh.devices.reshape(4, 2, 2, 16, 2), ROWS + COLS)
    by_cols, by_rows = P(COLS, ROWS), P(ROWS, COLS)
    in_specs = (
        by_cols,
        by_rows,
        by_rows,
        by_cols,
        by_cols,
        by_rows,
        by_rows,
        by_cols,
        by_rows,
        by_cols,
    )
    out_specs = (by_rows, by_cols, by_rows, by_cols)
    return jax.shard_map(local, mesh=parts, in_specs=in_specs, out_specs=out_specs, check_vma=False)
```

```python
import jax
import jax.numpy as jnp
from jax import lax
from jax.sharding import Mesh
from jax.sharding import PartitionSpec as P

QBLOCK = 32
ROWS = ("x", "yl")
COLS = ("yh", "z", "c")
SWAP = ((0, 1), (1, 0))


def restore(code, scale):
    count, width = code.shape
    blocks = code.astype(jnp.float32).reshape(count, width // QBLOCK, QBLOCK) * scale[:, :, None]
    return blocks.reshape(count, width).astype(jnp.bfloat16)


def dot_nt(left, right):
    return lax.dot_general(
        left, right, (((1,), (1,)), ((), ())), preferred_element_type=jnp.float32
    )


def dot_tn(left, right):
    return lax.dot_general(
        left, right, (((0,), (0,)), ((), ())), preferred_element_type=jnp.float32
    )


def local(
    grad_out,
    ctx_code,
    ctx_scale,
    stream_code,
    stream_scale,
    hidden_code,
    hidden_scale,
    out_weight,
    up_weight,
    down_weight,
):
    core = lax.axis_index("c")
    n_rows, n_z = lax.axis_size(ROWS), lax.axis_size("z")
    per = grad_out.shape[0]
    runs = n_z * 2 // n_rows
    features = grad_out.shape[1]

    def own_first(block):
        width = block.shape[1]
        parts = block.reshape(runs, 2, per, width)
        one, two = parts[:, 0], parts[:, 1]
        first = jnp.where(core == 0, one, two)
        second = jnp.where(core == 0, two, one)
        return jnp.stack([first, second]).reshape(block.shape)

    def natural(block):
        width = block.shape[1]
        parts = block.reshape(2, runs, per, width)
        one = jnp.where(core == 0, parts[0], parts[1])
        two = jnp.where(core == 0, parts[1], parts[0])
        return jnp.stack([one, two], axis=1).reshape(block.shape)

    def swap(block, axis):
        return lax.ppermute(block, axis, SWAP)

    def scatter_rows(own, other):
        width = own.shape[1]
        sent = jnp.stack([by_row(own), by_row(other)], axis=1)
        came = lax.all_to_all(sent, ROWS, 0, 0, tiled=True)
        return jnp.sum(came.astype(jnp.float32), axis=0).reshape(-1, width)

    def by_row(block):
        width = block.shape[1]
        parts = block.reshape(n_rows // 2, runs, 2, per, width)
        return parts.transpose(2, 0, 1, 3, 4).reshape(n_rows, runs * per, width)

    def by_z(block):
        width = block.shape[-1]
        parts = block.reshape(2, n_z, per, width)
        return jnp.swapaxes(parts, 0, 1).reshape(-1, width)

    def gather_z(pair):
        return lax.all_gather(pair.reshape(-1, features), "z", axis=0, tiled=True)

    def gather_rows(block):
        copies = lax.optimization_barrier(
            jnp.broadcast_to(block[None], (n_rows,) + block.shape)
        )
        every = lax.all_to_all(copies, ROWS, 0, 0, tiled=True)
        return every.reshape(n_rows, 2, -1, block.shape[1])

    stream = restore(stream_code, stream_scale)
    positive = jnp.maximum(
        own_first(restore(hidden_code, hidden_scale)).astype(jnp.float32), 0.0
    )
    act = (positive * positive).astype(jnp.bfloat16)
    context = own_first(restore(ctx_code, ctx_scale))
    hidden_width = act.shape[1]
    padding = jnp.zeros((act.shape[0], 512 - hidden_width - context.shape[1]), jnp.bfloat16)
    saved = jnp.concatenate([act, context, padding], axis=1)

    both = lax.all_gather(jnp.stack([grad_out, stream]), "yh", axis=0)
    stream_all = lax.all_gather(both[:, 1], ("z", "c"), axis=0)

    def first_half(pair):
        grad_own = gather_z(pair)
        grad_other = swap(grad_own, "c")
        grad_act = scatter_rows(
            dot_nt(grad_own, down_weight).astype(jnp.bfloat16),
            dot_nt(grad_other, down_weight).astype(jnp.bfloat16),
        )
        grad_pre = (grad_act * 2.0 * positive).astype(jnp.bfloat16)
        return grad_own, grad_other, gather_rows(grad_pre)

    def skip(pair):
        wide = jnp.zeros((n_z * 2 * per, features), jnp.bfloat16)
        return wide, wide, jnp.zeros((n_rows, 2, runs * per, hidden_width), jnp.bfloat16)

    always = lax.optimization_barrier(jnp.bool_(True))
    grad_own, grad_other, grad_pre_all = lax.cond(always, first_half, skip, both[:, 0])
    pre_own = by_z(grad_pre_all[:, 0])
    pre_other = by_z(grad_pre_all[:, 1])

    came = swap(dot_nt(pre_other, up_weight).astype(jnp.bfloat16), "c")
    part = (dot_nt(pre_own, up_weight) + came.astype(jnp.float32)).astype(jnp.bfloat16)
    pair_out = both[:, 0].reshape(2 * per, features).astype(jnp.float32)
    by_core = stream_all.reshape(n_z, 2, 2 * per, features)
    part, saved, by_core = lax.optimization_barrier((part, saved, by_core))
    saved_all = lax.all_gather(saved, ROWS, axis=0)

    def second_half(part, by_core):
        came = lax.all_to_all(part.reshape(n_z, 2 * per, features), "z", 0, 0, tiled=True)
        stream_own = lax.dynamic_index_in_dim(by_core, core, 1, keepdims=False)
        stream_other = lax.dynamic_index_in_dim(by_core, 1 - core, 1, keepdims=False)
        stream_own = stream_own.reshape(-1, features)
        stream_other = stream_other.reshape(-1, features)
        grad_up = dot_tn(stream_own, pre_own) + dot_tn(stream_other, pre_other)
        part = jnp.sum(came.astype(jnp.float32), axis=0).astype(jnp.bfloat16)
        summed = part.astype(jnp.float32) + swap(part, "yh").astype(jnp.float32)
        return (pair_out + summed).astype(jnp.bfloat16), grad_up

    def skip_second(part, by_core):
        return (
            jnp.zeros((2 * per, features), jnp.bfloat16),
            jnp.zeros((features, hidden_width), jnp.float32),
        )

    grad_stream, grad_up = lax.cond(always, second_half, skip_second, part, by_core)
    grad_stream, saved_all = lax.optimization_barrier((grad_stream, saved_all))

    gs_own = gather_z(grad_stream)
    gs_other = swap(gs_own, "c")
    grad_ctx = natural(
        scatter_rows(
            dot_nt(gs_own, out_weight).astype(jnp.bfloat16),
            dot_nt(gs_other, out_weight).astype(jnp.bfloat16),
        )
    ).astype(jnp.bfloat16)

    saved_pairs = saved_all.reshape(n_rows, 2, -1, saved_all.shape[-1])
    saved_own, saved_other = by_z(saved_pairs[:, 0]), by_z(saved_pairs[:, 1])
    act_own, act_other = saved_own[:, :hidden_width], saved_other[:, :hidden_width]
    ctx_own = saved_own[:, hidden_width : hidden_width + context.shape[1]]
    ctx_other = saved_other[:, hidden_width : hidden_width + context.shape[1]]
    grad_down = dot_tn(act_own, grad_own) + dot_tn(act_other, grad_other)
    grad_outw = dot_tn(ctx_own, gs_own) + dot_tn(ctx_other, gs_other)
    return (grad_ctx, grad_outw, grad_up, grad_down)


def solution(mesh):
    parts = Mesh(mesh.devices.reshape(4, 2, 2, 16, 2), ROWS + COLS)
    by_cols, by_rows = P(COLS, ROWS), P(ROWS, COLS)
    in_specs = (
        by_cols,
        by_rows,
        by_rows,
        by_cols,
        by_cols,
        by_rows,
        by_rows,
        by_cols,
        by_rows,
        by_cols,
    )
    out_specs = (by_rows, by_cols, by_rows, by_cols)
    return jax.shard_map(local, mesh=parts, in_specs=in_specs, out_specs=out_specs, check_vma=False)
```

```python
import jax
import jax.numpy as jnp
from jax import lax
from jax.sharding import Mesh
from jax.sharding import PartitionSpec as P

QBLOCK = 32
ROWS = ("x", "yl")
COLS = ("yh", "z", "c")
SWAP = ((0, 1), (1, 0))


def restore(code, scale):
    count, width = code.shape
    blocks = code.astype(jnp.float32).reshape(count, width // QBLOCK, QBLOCK) * scale[:, :, None]
    return blocks.reshape(count, width).astype(jnp.bfloat16)


def dot_nt(left, right):
    return lax.dot_general(
        left, right, (((1,), (1,)), ((), ())), preferred_element_type=jnp.float32
    )


def dot_tn(left, right):
    return lax.dot_general(
        left, right, (((0,), (0,)), ((), ())), preferred_element_type=jnp.float32
    )


def local(
    grad_out,
    ctx_code,
    ctx_scale,
    stream_code,
    stream_scale,
    hidden_code,
    hidden_scale,
    out_weight,
    up_weight,
    down_weight,
):
    core = lax.axis_index("c")
    half = lax.axis_index("yh")
    n_rows, n_z = lax.axis_size(ROWS), lax.axis_size("z")
    per = grad_out.shape[0]
    runs = n_z * 2 // n_rows
    features = grad_out.shape[1]

    def own_first(block):
        width = block.shape[1]
        parts = block.reshape(runs, 2, per, width)
        one, two = parts[:, 0], parts[:, 1]
        first = jnp.where(core == 0, one, two)
        second = jnp.where(core == 0, two, one)
        return jnp.stack([first, second]).reshape(block.shape)

    def natural(block):
        width = block.shape[1]
        parts = block.reshape(2, runs, per, width)
        one = jnp.where(core == 0, parts[0], parts[1])
        two = jnp.where(core == 0, parts[1], parts[0])
        return jnp.stack([one, two], axis=1).reshape(block.shape)

    def swap(block, axis):
        return lax.ppermute(block, axis, SWAP)

    def blocks_of(own, other):
        return jnp.stack([by_row(own), by_row(other)], axis=1)

    def scatter_rows(sent):
        came = lax.all_to_all(sent, ROWS, 0, 0, tiled=True)
        return jnp.sum(came.astype(jnp.float32), axis=0).reshape(-1, sent.shape[-1])

    def by_row(block):
        width = block.shape[1]
        parts = block.reshape(n_rows // 2, runs, 2, per, width)
        return parts.transpose(2, 0, 1, 3, 4).reshape(n_rows, runs * per, width)

    def by_z(block):
        width = block.shape[-1]
        parts = block.reshape(2, n_z, per, width)
        return jnp.swapaxes(parts, 0, 1).reshape(-1, width)

    def gather_z(pair):
        return lax.all_gather(pair.reshape(-1, features), "z", axis=0, tiled=True)

    def gather_rows(block):
        copies = lax.optimization_barrier(
            jnp.broadcast_to(block[None], (n_rows,) + block.shape)
        )
        every = lax.all_to_all(copies, ROWS, 0, 0, tiled=True)
        return every.reshape(n_rows, 2, -1, block.shape[1])

    stream = restore(stream_code, stream_scale)
    positive = jnp.maximum(
        own_first(restore(hidden_code, hidden_scale)).astype(jnp.float32), 0.0
    )
    act = (positive * positive).astype(jnp.bfloat16)
    context = own_first(restore(ctx_code, ctx_scale))
    hidden_width = act.shape[1]
    padding = jnp.zeros((act.shape[0], 512 - hidden_width - context.shape[1]), jnp.bfloat16)
    saved = jnp.concatenate([act, context, padding], axis=1)

    both = lax.all_gather(jnp.stack([grad_out, stream]), "yh", axis=0)
    stream_all = lax.all_gather(both[:, 1], ("z", "c"), axis=0)

    def first_half(both):
        grad_own = gather_z(both[:, 0])
        grad_other = swap(grad_own, "c")
        sent = blocks_of(
            dot_nt(grad_own, down_weight).astype(jnp.bfloat16),
            dot_nt(grad_other, down_weight).astype(jnp.bfloat16),
        )
        grad_act = scatter_rows(sent)
        grad_pre = (grad_act * 2.0 * positive).astype(jnp.bfloat16)
        return grad_own, grad_other, gather_rows(grad_pre)

    def skip(both):
        wide = jnp.zeros((n_z * 2 * per, features), jnp.bfloat16)
        return wide, wide, jnp.zeros((n_rows, 2, runs * per, hidden_width), jnp.bfloat16)

    always = lax.optimization_barrier(jnp.bool_(True))
    grad_own, grad_other, grad_pre_all = lax.cond(always, first_half, skip, both)
    pre_own = by_z(grad_pre_all[:, 0])
    pre_other = by_z(grad_pre_all[:, 1])

    came = swap(dot_nt(pre_other, up_weight).astype(jnp.bfloat16), "c")
    part = (dot_nt(pre_own, up_weight) + came.astype(jnp.float32)).reshape(n_z, 2, per, features)
    keep = lax.dynamic_index_in_dim(part, half, 1, keepdims=False)
    send = lax.dynamic_index_in_dim(part, 1 - half, 1, keepdims=False).astype(jnp.bfloat16)
    by_core = stream_all.reshape(n_z, 2, 2 * per, features)
    send, saved, by_core = lax.optimization_barrier((send, saved, by_core))
    saved_all = lax.all_gather(saved, ROWS, axis=0)

    def second_half(keep, send, by_core):
        part = (keep + swap(send, "yh").astype(jnp.float32)).astype(jnp.bfloat16)
        came = lax.all_to_all(part, "z", 0, 0, tiled=True)
        stream_own = lax.dynamic_index_in_dim(by_core, core, 1, keepdims=False)
        stream_other = lax.dynamic_index_in_dim(by_core, 1 - core, 1, keepdims=False)
        stream_own = stream_own.reshape(-1, features)
        stream_other = stream_other.reshape(-1, features)
        grad_up = dot_tn(stream_own, pre_own) + dot_tn(stream_other, pre_other)
        summed = jnp.sum(came.astype(jnp.float32), axis=0)
        grad_stream = (grad_out.astype(jnp.float32) + summed).astype(jnp.bfloat16)
        return lax.all_gather(grad_stream, "yh", axis=0), grad_up

    def skip_second(keep, send, by_core):
        return (
            jnp.zeros((2, per, features), jnp.bfloat16),
            jnp.zeros((features, hidden_width), jnp.float32),
        )

    grad_stream, grad_up = lax.cond(always, second_half, skip_second, keep, send, by_core)
    grad_stream, saved_all = lax.optimization_barrier((grad_stream, saved_all))

    gs_own = gather_z(grad_stream)
    gs_other = swap(gs_own, "c")
    ctx_width = out_weight.shape[0]
    wide = jnp.pad(out_weight, ((0, -ctx_width % 128), (0, 0)))
    sent = blocks_of(
        dot_nt(gs_own, wide).astype(jnp.bfloat16), dot_nt(gs_other, wide).astype(jnp.bfloat16)
    )
    sent, saved_all = lax.optimization_barrier((sent, saved_all))
    grad_ctx = natural(scatter_rows(sent)[:, :ctx_width].astype(jnp.bfloat16))

    saved_pairs = saved_all.reshape(n_rows, 2, -1, saved_all.shape[-1])
    saved_own, saved_other = by_z(saved_pairs[:, 0]), by_z(saved_pairs[:, 1])
    act_own, act_other = saved_own[:, :hidden_width], saved_other[:, :hidden_width]
    ctx_own = saved_own[:, hidden_width : hidden_width + ctx_width]
    ctx_other = saved_other[:, hidden_width : hidden_width + ctx_width]
    grad_down = dot_tn(act_own, grad_own) + dot_tn(act_other, grad_other)
    grad_outw = dot_tn(ctx_own, gs_own) + dot_tn(ctx_other, gs_other)
    return (grad_ctx, grad_outw, grad_up, grad_down)


def solution(mesh):
    parts = Mesh(mesh.devices.reshape(4, 2, 2, 16, 2), ROWS + COLS)
    by_cols, by_rows = P(COLS, ROWS), P(ROWS, COLS)
    in_specs = (
        by_cols,
        by_rows,
        by_rows,
        by_cols,
        by_cols,
        by_rows,
        by_rows,
        by_cols,
        by_rows,
        by_cols,
    )
    out_specs = (by_rows, by_cols, by_rows, by_cols)
    return jax.shard_map(local, mesh=parts, in_specs=in_specs, out_specs=out_specs, check_vma=False)
```

```python
import jax
import jax.numpy as jnp
from jax import lax
from jax.experimental import pallas as pl
from jax.experimental.pallas import tpu as pltpu
from jax.sharding import Mesh
from jax.sharding import PartitionSpec as P

QBLOCK = 32
PER = 16
ROWS = ("x", "yl")
COLS = ("yh", "z", "c")
SWAP = ((0, 1), (1, 0))


def restore(code, scale):
    count, width = code.shape
    blocks = code.astype(jnp.float32).reshape(count, width // QBLOCK, QBLOCK) * scale[:, :, None]
    return blocks.reshape(count, width).astype(jnp.bfloat16)


def dot_nt(left, right):
    return lax.dot_general(
        left, right, (((1,), (1,)), ((), ())), preferred_element_type=jnp.float32
    )


def dot_tn(left, right):
    return lax.dot_general(
        left, right, (((0,), (0,)), ((), ())), preferred_element_type=jnp.float32
    )


def outgoing_kernel(grad_ref, code_ref, scale_ref, out_ref):
    blocks, width = scale_ref.shape[1], code_ref.shape[1]
    row = lax.broadcasted_iota(jnp.int32, (blocks, width), 0)
    column = lax.broadcasted_iota(jnp.int32, (blocks, width), 1)
    first = row * QBLOCK
    spread = jnp.where((column >= first) & (column < first + QBLOCK), 1.0, 0.0)
    scale = jnp.dot(
        scale_ref[...],
        spread.astype(jnp.float32),
        precision=lax.Precision.HIGHEST,
        preferred_element_type=jnp.float32,
    )
    out_ref[0] = grad_ref[...]
    out_ref[1] = (code_ref[...].astype(jnp.float32) * scale).astype(jnp.bfloat16)


def outgoing(grad_out, code, scale):
    return pl.pallas_call(
        outgoing_kernel,
        out_shape=jax.ShapeDtypeStruct((2,) + grad_out.shape, jnp.bfloat16),
        in_specs=[pl.BlockSpec(memory_space=pltpu.VMEM)] * 3,
        out_specs=pl.BlockSpec(memory_space=pltpu.VMEM),
    )(grad_out, code, scale)


def last_kernel(
    saved_ref, grad_own_ref, grad_other_ref, gs_own_ref, gs_other_ref, down_ref, out_ref, rows_ref
):
    n_rows, _, block, wide = saved_ref.shape
    runs, per = rows_ref.shape[0] * 2 // n_rows, rows_ref.shape[2]
    hidden_width, ctx_width = down_ref.shape[0], out_ref.shape[0]
    for side, grad_ref, gs_ref in (
        (0, grad_own_ref, gs_own_ref),
        (1, grad_other_ref, gs_other_ref),
    ):
        for row in range(n_rows):
            half, first = row // (n_rows // 2), row % (n_rows // 2) * runs
            for run in range(runs):
                rows_ref[first + run, half] = saved_ref[row, side, pl.ds(run * per, per), :]
        rows = rows_ref[...].reshape(-1, wide)
        down = dot_tn(rows[:, :hidden_width], grad_ref[...])
        out = dot_tn(rows[:, hidden_width:], gs_ref[...])[:ctx_width]
        if side == 0:
            down_ref[...] = down
            out_ref[...] = out
        else:
            down_ref[...] += down
            out_ref[...] += out


def last_products(saved_all, grad_own, grad_other, gs_own, gs_other, hidden_width, ctx_width):
    features = grad_own.shape[1]
    return pl.pallas_call(
        last_kernel,
        out_shape=(
            jax.ShapeDtypeStruct((hidden_width, features), jnp.float32),
            jax.ShapeDtypeStruct((ctx_width, features), jnp.float32),
        ),
        in_specs=[pl.BlockSpec(memory_space=pltpu.VMEM)] * 5,
        out_specs=(pl.BlockSpec(memory_space=pltpu.VMEM),) * 2,
        scratch_shapes=[
            pltpu.VMEM((grad_own.shape[0] // (2 * PER), 2, PER, saved_all.shape[3]), jnp.bfloat16)
        ],
        compiler_params=pltpu.CompilerParams(vmem_limit_bytes=32 * 2**20),
        cost_estimate=pl.CostEstimate(
            flops=4 * grad_own.size * saved_all.shape[3],
            bytes_accessed=8 * grad_own.size + 2 * saved_all.size,
            transcendentals=0,
        ),
    )(saved_all, grad_own, grad_other, gs_own, gs_other)


def local(
    grad_out,
    ctx_code,
    ctx_scale,
    stream_code,
    stream_scale,
    hidden_code,
    hidden_scale,
    out_weight,
    up_weight,
    down_weight,
):
    core = lax.axis_index("c")
    half = lax.axis_index("yh")
    n_rows, n_z = lax.axis_size(ROWS), lax.axis_size("z")
    per = grad_out.shape[0]
    runs = n_z * 2 // n_rows
    features = grad_out.shape[1]
    hidden_width, ctx_width = hidden_code.shape[1], ctx_code.shape[1]

    def own_first(block):
        width = block.shape[1]
        parts = block.reshape(runs, 2, per, width)
        one, two = parts[:, 0], parts[:, 1]
        first = jnp.where(core == 0, one, two)
        second = jnp.where(core == 0, two, one)
        return jnp.stack([first, second]).reshape(block.shape)

    def natural(block):
        width = block.shape[1]
        parts = block.reshape(2, runs, per, width)
        one = jnp.where(core == 0, parts[0], parts[1])
        two = jnp.where(core == 0, parts[1], parts[0])
        return jnp.stack([one, two], axis=1).reshape(block.shape)

    def swap(block, axis):
        return lax.ppermute(block, axis, SWAP)

    def blocks_of(own, other):
        return jnp.stack([by_row(own), by_row(other)], axis=1)

    def scatter_rows(sent):
        came = lax.all_to_all(sent, ROWS, 0, 0, tiled=True)
        return jnp.sum(came.astype(jnp.float32), axis=0).reshape(-1, sent.shape[-1])

    def by_row(block):
        width = block.shape[1]
        parts = block.reshape(n_rows // 2, runs, 2, per, width)
        return parts.transpose(2, 0, 1, 3, 4).reshape(n_rows, runs * per, width)

    def by_z(block):
        width = block.shape[-1]
        parts = block.reshape(2, n_z, per, width)
        return jnp.swapaxes(parts, 0, 1).reshape(-1, width)

    def gather_z(pair):
        return lax.all_gather(pair.reshape(-1, features), "z", axis=0, tiled=True)

    def gather_rows(block):
        copies = lax.optimization_barrier(
            jnp.broadcast_to(block[None], (n_rows,) + block.shape)
        )
        every = lax.all_to_all(copies, ROWS, 0, 0, tiled=True)
        return every.reshape(n_rows, 2, -1, block.shape[1])

    both = lax.all_gather(outgoing(grad_out, stream_code, stream_scale), "yh", axis=0)
    stream_all = lax.all_gather(both[:, 1], ("z", "c"), axis=0)

    def first_half(both):
        grad_own = gather_z(both[:, 0])
        grad_other = swap(grad_own, "c")
        sent = blocks_of(
            dot_nt(grad_own, down_weight).astype(jnp.bfloat16),
            dot_nt(grad_other, down_weight).astype(jnp.bfloat16),
        )
        grad_act = scatter_rows(sent)
        positive = jnp.maximum(
            own_first(restore(hidden_code, hidden_scale)).astype(jnp.float32), 0.0
        )
        act = (positive * positive).astype(jnp.bfloat16)
        grad_pre = (grad_act * 2.0 * positive).astype(jnp.bfloat16)
        return grad_own, grad_other, gather_rows(grad_pre), act

    def skip(both):
        wide = jnp.zeros((n_z * 2 * per, features), jnp.bfloat16)
        pre = jnp.zeros((n_rows, 2, runs * per, hidden_width), jnp.bfloat16)
        return wide, wide, pre, jnp.zeros(hidden_code.shape, jnp.bfloat16)

    always = lax.optimization_barrier(jnp.bool_(True))
    grad_own, grad_other, grad_pre_all, act = lax.cond(always, first_half, skip, both)
    context = own_first(restore(ctx_code, ctx_scale))
    padding = jnp.zeros((act.shape[0], 512 - hidden_width - ctx_width), jnp.bfloat16)
    saved = jnp.concatenate([act, context, padding], axis=1)
    pre_own = by_z(grad_pre_all[:, 0])
    pre_other = by_z(grad_pre_all[:, 1])

    came = swap(dot_nt(pre_other, up_weight).astype(jnp.bfloat16), "c")
    part = (dot_nt(pre_own, up_weight) + came.astype(jnp.float32)).reshape(n_z, 2, per, features)
    keep = lax.dynamic_index_in_dim(part, half, 1, keepdims=False)
    send = lax.dynamic_index_in_dim(part, 1 - half, 1, keepdims=False).astype(jnp.bfloat16)
    by_core = stream_all.reshape(n_z, 2, 2 * per, features)
    part = (keep + swap(send, "yh").astype(jnp.float32)).astype(jnp.bfloat16)
    part, saved, by_core = lax.optimization_barrier((part, saved, by_core))
    saved_all = lax.all_gather(saved, ROWS, axis=0)
    padded_out = jnp.pad(out_weight, ((0, -ctx_width % 128), (0, 0)))

    def second_half(part, by_core):
        came = lax.all_to_all(part, "z", 0, 0, tiled=True)
        stream_own = lax.dynamic_index_in_dim(by_core, core, 1, keepdims=False)
        stream_other = lax.dynamic_index_in_dim(by_core, 1 - core, 1, keepdims=False)
        stream_own = stream_own.reshape(-1, features)
        stream_other = stream_other.reshape(-1, features)
        grad_up = dot_tn(stream_own, pre_own) + dot_tn(stream_other, pre_other)
        summed = jnp.sum(came.astype(jnp.float32), axis=0)
        grad_stream = (grad_out.astype(jnp.float32) + summed).astype(jnp.bfloat16)
        gs_own = gather_z(lax.all_gather(grad_stream, "yh", axis=0))
        gs_other = swap(gs_own, "c")
        sent = blocks_of(
            dot_nt(gs_own, padded_out).astype(jnp.bfloat16),
            dot_nt(gs_other, padded_out).astype(jnp.bfloat16),
        )
        return gs_own, gs_other, sent, grad_up

    def skip_second(part, by_core):
        wide = jnp.zeros((n_z * 2 * per, features), jnp.bfloat16)
        return (
            wide,
            wide,
            jnp.zeros((n_rows, 2, runs * per, padded_out.shape[0]), jnp.bfloat16),
            jnp.zeros((features, hidden_width), jnp.float32),
        )

    gs_own, gs_other, sent, grad_up = lax.cond(always, second_half, skip_second, part, by_core)
    sent, saved_all = lax.optimization_barrier((sent, saved_all))
    grad_ctx = natural(scatter_rows(sent)[:, :ctx_width].astype(jnp.bfloat16))
    grad_down, grad_outw = last_products(
        saved_all.reshape(n_rows, 2, -1, saved_all.shape[-1]),
        grad_own,
        grad_other,
        gs_own,
        gs_other,
        hidden_width,
        ctx_width,
    )
    return (grad_ctx, grad_outw, grad_up, grad_down)


def solution(mesh):
    parts = Mesh(mesh.devices.reshape(4, 2, 2, 16, 2), ROWS + COLS)
    by_cols, by_rows = P(COLS, ROWS), P(ROWS, COLS)
    in_specs = (
        by_cols,
        by_rows,
        by_rows,
        by_cols,
        by_cols,
        by_rows,
        by_rows,
        by_cols,
        by_rows,
        by_cols,
    )
    out_specs = (by_rows, by_cols, by_rows, by_cols)
    return jax.shard_map(local, mesh=parts, in_specs=in_specs, out_specs=out_specs, check_vma=False)
```

```python
import jax
import jax.numpy as jnp
from jax import lax
from jax.experimental import pallas as pl
from jax.experimental.pallas import tpu as pltpu
from jax.sharding import Mesh
from jax.sharding import PartitionSpec as P

QBLOCK = 32
PER = 16
ROWS = ("x", "yl")
COLS = ("yh", "z", "c")
SWAP = ((0, 1), (1, 0))


def restore(code, scale):
    count, width = code.shape
    blocks = code.astype(jnp.float32).reshape(count, width // QBLOCK, QBLOCK) * scale[:, :, None]
    return blocks.reshape(count, width).astype(jnp.bfloat16)


def dot_nt(left, right):
    return lax.dot_general(
        left, right, (((1,), (1,)), ((), ())), preferred_element_type=jnp.float32
    )


def dot_tn(left, right):
    return lax.dot_general(
        left, right, (((0,), (0,)), ((), ())), preferred_element_type=jnp.float32
    )


def outgoing_kernel(grad_ref, code_ref, scale_ref, out_ref):
    blocks, width = scale_ref.shape[1], code_ref.shape[1]
    row = lax.broadcasted_iota(jnp.int32, (blocks, width), 0)
    column = lax.broadcasted_iota(jnp.int32, (blocks, width), 1)
    first = row * QBLOCK
    spread = jnp.where((column >= first) & (column < first + QBLOCK), 1.0, 0.0)
    scale = jnp.dot(
        scale_ref[...],
        spread.astype(jnp.float32),
        precision=lax.Precision.HIGHEST,
        preferred_element_type=jnp.float32,
    )
    out_ref[0] = grad_ref[...]
    out_ref[1] = (code_ref[...].astype(jnp.float32) * scale).astype(jnp.bfloat16)


def outgoing(grad_out, code, scale):
    return pl.pallas_call(
        outgoing_kernel,
        out_shape=jax.ShapeDtypeStruct((2,) + grad_out.shape, jnp.bfloat16),
        in_specs=[pl.BlockSpec(memory_space=pltpu.VMEM)] * 3,
        out_specs=pl.BlockSpec(memory_space=pltpu.VMEM),
    )(grad_out, code, scale)


def last_kernel(
    saved_ref, grad_own_ref, grad_other_ref, gs_own_ref, gs_other_ref, down_ref, out_ref, rows_ref
):
    n_rows, _, block, wide = saved_ref.shape
    runs, per = rows_ref.shape[0] * 2 // n_rows, rows_ref.shape[2]
    hidden_width = down_ref.shape[0]
    for side, grad_ref, gs_ref in (
        (0, grad_own_ref, gs_own_ref),
        (1, grad_other_ref, gs_other_ref),
    ):
        for row in range(n_rows):
            half, first = row // (n_rows // 2), row % (n_rows // 2) * runs
            for run in range(runs):
                rows_ref[first + run, half] = saved_ref[row, side, pl.ds(run * per, per), :]
        rows = rows_ref[...].reshape(-1, wide)
        down = dot_tn(rows[:, :hidden_width], grad_ref[...])
        out = dot_tn(rows[:, hidden_width:], gs_ref[...])
        if side == 0:
            down_ref[...] = down
            out_ref[...] = out
        else:
            down_ref[...] += down
            out_ref[...] += out


def last_products(saved_all, grad_own, grad_other, gs_own, gs_other, hidden_width):
    features = grad_own.shape[1]
    return pl.pallas_call(
        last_kernel,
        out_shape=(
            jax.ShapeDtypeStruct((hidden_width, features), jnp.float32),
            jax.ShapeDtypeStruct((saved_all.shape[3] - hidden_width, gs_own.shape[1]), jnp.float32),
        ),
        in_specs=[pl.BlockSpec(memory_space=pltpu.VMEM)] * 5,
        out_specs=(pl.BlockSpec(memory_space=pltpu.VMEM),) * 2,
        scratch_shapes=[
            pltpu.VMEM((grad_own.shape[0] // (2 * PER), 2, PER, saved_all.shape[3]), jnp.bfloat16)
        ],
        compiler_params=pltpu.CompilerParams(vmem_limit_bytes=32 * 2**20),
        cost_estimate=pl.CostEstimate(
            flops=4 * grad_own.size * hidden_width,
            bytes_accessed=8 * grad_own.size + 2 * saved_all.size,
            transcendentals=0,
        ),
    )(saved_all, grad_own, grad_other, gs_own, gs_other)


def local(
    grad_out,
    ctx_code,
    ctx_scale,
    stream_code,
    stream_scale,
    hidden_code,
    hidden_scale,
    out_weight,
    up_weight,
    down_weight,
):
    core, half = lax.axis_index("c"), lax.axis_index("yh")
    n_rows, n_z = lax.axis_size(ROWS), lax.axis_size("z")
    per, features = grad_out.shape
    runs = n_z * 2 // n_rows
    hidden_width, ctx_width = hidden_code.shape[1], ctx_code.shape[1]
    span = features // 2
    padded = ctx_width + -ctx_width % 128

    def own_first(block):
        width = block.shape[1]
        parts = block.reshape(runs, 2, per, width)
        one, two = parts[:, 0], parts[:, 1]
        first = jnp.where(core == 0, one, two)
        second = jnp.where(core == 0, two, one)
        return jnp.stack([first, second]).reshape(block.shape)

    def natural(block):
        width = block.shape[1]
        parts = block.reshape(2, runs, per, width)
        one = jnp.where(core == 0, parts[0], parts[1])
        two = jnp.where(core == 0, parts[1], parts[0])
        return jnp.stack([one, two], axis=1).reshape(block.shape)

    def swap(block, axis):
        return lax.ppermute(block, axis, SWAP)

    def by_half(mine, theirs):
        return jnp.where(half == 0, mine, theirs), jnp.where(half == 0, theirs, mine)

    def columns(block, which):
        return lax.dynamic_slice_in_dim(block, which * span, span, axis=1)

    def by_row(block):
        width = block.shape[1]
        parts = block.reshape(n_rows // 2, runs, 2, per, width)
        return parts.transpose(2, 0, 1, 3, 4).reshape(n_rows, runs * per, width)

    def by_z(block):
        width = block.shape[-1]
        parts = block.reshape(2, n_z, per, width)
        return jnp.swapaxes(parts, 0, 1).reshape(-1, width)

    def summed(came):
        return jnp.sum(came.astype(jnp.float32), axis=0)

    both = lax.all_gather(outgoing(grad_out, stream_code, stream_scale), "yh", axis=0)
    stream_all = lax.all_gather(both[:, 1], ("z", "c"), axis=0)

    def first_half(both):
        context = own_first(restore(ctx_code, ctx_scale))
        grad_own = lax.all_gather(both[:, 0].reshape(-1, features), "z", axis=0, tiled=True)
        grad_other = swap(grad_own, "c")
        up_sent = lax.dynamic_slice_in_dim(up_weight, (1 - half) * span, span, axis=0)
        wide_ctx = jnp.pad(context, ((0, 0), (0, hidden_width - ctx_width)))
        sent = jnp.concatenate([up_sent, columns(out_weight, 1 - half), wide_ctx])
        swapped = swap(sent, "yh")
        sent = jnp.stack(
            [
                by_row(dot_nt(grad_own, down_weight).astype(jnp.bfloat16)),
                by_row(dot_nt(grad_other, down_weight).astype(jnp.bfloat16)),
            ],
            axis=1,
        )
        grad_act = summed(lax.all_to_all(sent, ROWS, 0, 0, tiled=True)).reshape(-1, hidden_width)
        grad_act, swapped = lax.optimization_barrier((grad_act, swapped))
        positive = jnp.maximum(
            own_first(restore(hidden_code, hidden_scale)).astype(jnp.float32), 0.0
        )
        act = (positive * positive).astype(jnp.bfloat16)
        grad_pre = (grad_act * 2.0 * positive).astype(jnp.bfloat16)
        copies = lax.optimization_barrier(
            jnp.broadcast_to(grad_pre[None], (2 * n_rows,) + grad_pre.shape)
        )
        pre_all = lax.all_to_all(copies, ROWS + ("yh",), 0, 0, tiled=True)
        pre_all = pre_all.reshape(n_rows, 2, 2, runs * per, hidden_width)
        return grad_own, grad_other, pre_all, act, context, swapped

    def skip_first(both):
        wide = jnp.zeros((n_z * 2 * per, features), jnp.bfloat16)
        pre_all = jnp.zeros((n_rows, 2, 2, runs * per, hidden_width), jnp.bfloat16)
        act = jnp.zeros(hidden_code.shape, jnp.bfloat16)
        swapped = jnp.zeros((span + ctx_width + act.shape[0], hidden_width), jnp.bfloat16)
        return wide, wide, pre_all, act, jnp.zeros(ctx_code.shape, jnp.bfloat16), swapped

    always = lax.optimization_barrier(jnp.bool_(True))
    grad_own, grad_other, pre_all, act, context, swapped = lax.cond(
        always, first_half, skip_first, both
    )
    up_kept = lax.dynamic_slice_in_dim(up_weight, half * span, span, axis=0)
    up_halves = by_half(up_kept, swapped[:span])
    out_halves = by_half(columns(out_weight, half), swapped[span : span + ctx_width])
    ctx_swapped = swapped[span + ctx_width :, :ctx_width]
    gap = ((0, 0), (0, padded - ctx_width))
    saved = jnp.concatenate([act, jnp.pad(context, gap), jnp.pad(ctx_swapped, gap)], axis=1)
    out_wide = jnp.concatenate(
        [jnp.pad(part, ((0, padded - ctx_width), (0, 0))) for part in out_halves]
    )

    def stream_part(side):
        one = pre_all[:, 0, side].reshape(-1, hidden_width)
        two = pre_all[:, 1, side].reshape(-1, hidden_width)
        return dot_nt(one, up_halves[0]) + dot_nt(two, up_halves[1])

    came = swap(stream_part(1).astype(jnp.bfloat16), "c")
    part = by_z((stream_part(0) + came.astype(jnp.float32)).astype(jnp.bfloat16))
    by_core = stream_all.reshape(n_z, 2, 2 * per, features)
    part, saved, by_core = lax.optimization_barrier((part, saved, by_core))
    saved_all = lax.all_gather(saved, ROWS, axis=0)
    kept_out = columns(both[:, 0].reshape(-1, features), half).astype(jnp.float32)

    def second_half(part, by_core):
        came = lax.all_to_all(part.reshape(n_z, 2 * per, span), "z", 0, 0, tiled=True)
        stream_own = lax.dynamic_index_in_dim(by_core, core, 1, keepdims=False)
        stream_other = lax.dynamic_index_in_dim(by_core, 1 - core, 1, keepdims=False)
        pre = lax.dynamic_index_in_dim(pre_all, half, 1, keepdims=False)
        grad_up = dot_tn(stream_own.reshape(-1, features), by_z(pre[:, 0])) + dot_tn(
            stream_other.reshape(-1, features), by_z(pre[:, 1])
        )
        came, grad_up = lax.optimization_barrier((came, grad_up))
        grad_stream = (kept_out + summed(came)).astype(jnp.bfloat16)
        gs_own = lax.all_gather(grad_stream, "z", axis=0, tiled=True)
        gs_other = swap(gs_own, "c")
        sides = [
            by_row(dot_nt(rows, out_wide).astype(jnp.bfloat16)).reshape(n_rows, -1, 2, padded)
            for rows in (gs_own, gs_other)
        ]
        sent = jnp.stack([jnp.swapaxes(side, 1, 2) for side in sides], axis=2)
        return gs_own, gs_other, sent, grad_up

    def skip_second(part, by_core):
        wide = jnp.zeros((n_z * 2 * per, span), jnp.bfloat16)
        return (
            wide,
            wide,
            jnp.zeros((n_rows, 2, 2, runs * per, padded), jnp.bfloat16),
            jnp.zeros((features, hidden_width), jnp.float32),
        )

    gs_own, gs_other, sent, grad_up = lax.cond(always, second_half, skip_second, part, by_core)
    sent, saved_all = lax.optimization_barrier((sent, saved_all))
    sent = sent.reshape(2 * n_rows, 2, runs * per, padded)
    came = summed(lax.all_to_all(sent, ROWS + ("yh",), 0, 0, tiled=True)).reshape(-1, padded)
    grad_ctx = natural(came[:, :ctx_width].astype(jnp.bfloat16))

    def weights(saved_all):
        grad_down, products = last_products(
            saved_all.reshape(n_rows, 2, -1, saved_all.shape[-1]),
            grad_own,
            grad_other,
            gs_own,
            gs_other,
            hidden_width,
        )
        mine = products[:ctx_width]
        theirs = swap(products[padded : padded + ctx_width], "yh")
        return grad_down, jnp.concatenate(by_half(mine, theirs), axis=1)

    def skip_weights(saved_all):
        return (
            jnp.zeros((hidden_width, features), jnp.float32),
            jnp.zeros((ctx_width, features), jnp.float32),
        )

    grad_down, grad_outw = lax.cond(always, weights, skip_weights, saved_all)
    return (grad_ctx, grad_outw, grad_up, grad_down)


def solution(mesh):
    parts = Mesh(mesh.devices.reshape(4, 2, 2, 16, 2), ROWS + COLS)
    by_cols, by_rows = P(COLS, ROWS), P(ROWS, COLS)
    in_specs = (
        by_cols,
        by_rows,
        by_rows,
        by_cols,
        by_cols,
        by_rows,
        by_rows,
        by_cols,
        by_rows,
        by_cols,
    )
    out_specs = (by_rows, by_cols, by_rows, by_cols)
    return jax.shard_map(local, mesh=parts, in_specs=in_specs, out_specs=out_specs, check_vma=False)
```

```python
import jax
import jax.numpy as jnp
from jax import lax
from jax.experimental import pallas as pl
from jax.experimental.pallas import tpu as pltpu
from jax.sharding import Mesh
from jax.sharding import PartitionSpec as P

QBLOCK = 32
PER = 16
ROWS = ("x", "yl")
COLS = ("yh", "z", "c")
SWAP = ((0, 1), (1, 0))


def restore(code, scale):
    count, width = code.shape
    blocks = code.astype(jnp.float32).reshape(count, width // QBLOCK, QBLOCK) * scale[:, :, None]
    return blocks.reshape(count, width).astype(jnp.bfloat16)


def dot_nt(left, right):
    return lax.dot_general(
        left, right, (((1,), (1,)), ((), ())), preferred_element_type=jnp.float32
    )


def dot_tn(left, right):
    return lax.dot_general(
        left, right, (((0,), (0,)), ((), ())), preferred_element_type=jnp.float32
    )


def outgoing_kernel(grad_ref, code_ref, scale_ref, out_ref):
    blocks, width = scale_ref.shape[1], code_ref.shape[1]
    row = lax.broadcasted_iota(jnp.int32, (blocks, width), 0)
    column = lax.broadcasted_iota(jnp.int32, (blocks, width), 1)
    first = row * QBLOCK
    spread = jnp.where((column >= first) & (column < first + QBLOCK), 1.0, 0.0)
    scale = jnp.dot(
        scale_ref[...],
        spread.astype(jnp.float32),
        precision=lax.Precision.HIGHEST,
        preferred_element_type=jnp.float32,
    )
    out_ref[0] = grad_ref[...]
    out_ref[1] = (code_ref[...].astype(jnp.float32) * scale).astype(jnp.bfloat16)


def outgoing(grad_out, code, scale):
    return pl.pallas_call(
        outgoing_kernel,
        out_shape=jax.ShapeDtypeStruct((2,) + grad_out.shape, jnp.bfloat16),
        in_specs=[pl.BlockSpec(memory_space=pltpu.VMEM)] * 3,
        out_specs=pl.BlockSpec(memory_space=pltpu.VMEM),
    )(grad_out, code, scale)


def last_kernel(
    saved_ref, grad_own_ref, grad_other_ref, gs_own_ref, gs_other_ref, down_ref, out_ref, rows_ref
):
    n_rows, _, block, wide = saved_ref.shape
    runs, per = rows_ref.shape[0] * 2 // n_rows, rows_ref.shape[2]
    hidden_width, ctx_width = down_ref.shape[0], out_ref.shape[0]
    for side, grad_ref, gs_ref in (
        (0, grad_own_ref, gs_own_ref),
        (1, grad_other_ref, gs_other_ref),
    ):
        for row in range(n_rows):
            half, first = row // (n_rows // 2), row % (n_rows // 2) * runs
            for run in range(runs):
                rows_ref[first + run, half] = saved_ref[row, side, pl.ds(run * per, per), :]
        rows = rows_ref[...].reshape(-1, wide)
        down = dot_tn(rows[:, :hidden_width], grad_ref[...])
        out = dot_tn(rows[:, hidden_width:], gs_ref[...])[:ctx_width]
        if side == 0:
            down_ref[...] = down
            out_ref[...] = out
        else:
            down_ref[...] += down
            out_ref[...] += out


def last_products(saved_all, grad_own, grad_other, gs_own, gs_other, hidden_width, ctx_width):
    features = grad_own.shape[1]
    return pl.pallas_call(
        last_kernel,
        out_shape=(
            jax.ShapeDtypeStruct((hidden_width, features), jnp.float32),
            jax.ShapeDtypeStruct((ctx_width, features), jnp.float32),
        ),
        in_specs=[pl.BlockSpec(memory_space=pltpu.VMEM)] * 5,
        out_specs=(pl.BlockSpec(memory_space=pltpu.VMEM),) * 2,
        scratch_shapes=[
            pltpu.VMEM((grad_own.shape[0] // (2 * PER), 2, PER, saved_all.shape[3]), jnp.bfloat16)
        ],
        compiler_params=pltpu.CompilerParams(vmem_limit_bytes=32 * 2**20),
        cost_estimate=pl.CostEstimate(
            flops=4 * grad_own.size * saved_all.shape[3],
            bytes_accessed=8 * grad_own.size + 2 * saved_all.size,
            transcendentals=0,
        ),
    )(saved_all, grad_own, grad_other, gs_own, gs_other)


def local(
    grad_out,
    ctx_code,
    ctx_scale,
    stream_code,
    stream_scale,
    hidden_code,
    hidden_scale,
    out_weight,
    up_weight,
    down_weight,
):
    core = lax.axis_index("c")
    half = lax.axis_index("yh")
    n_rows, n_z = lax.axis_size(ROWS), lax.axis_size("z")
    per = grad_out.shape[0]
    runs = n_z * 2 // n_rows
    features = grad_out.shape[1]
    hidden_width, ctx_width = hidden_code.shape[1], ctx_code.shape[1]

    def own_first(block):
        width = block.shape[1]
        parts = block.reshape(runs, 2, per, width)
        one, two = parts[:, 0], parts[:, 1]
        first = jnp.where(core == 0, one, two)
        second = jnp.where(core == 0, two, one)
        return jnp.stack([first, second]).reshape(block.shape)

    def natural(block):
        width = block.shape[1]
        parts = block.reshape(2, runs, per, width)
        one = jnp.where(core == 0, parts[0], parts[1])
        two = jnp.where(core == 0, parts[1], parts[0])
        return jnp.stack([one, two], axis=1).reshape(block.shape)

    def swap(block, axis):
        return lax.ppermute(block, axis, SWAP)

    def blocks_of(own, other):
        return jnp.stack([by_row(own), by_row(other)], axis=1)

    def scatter_rows(sent):
        came = lax.all_to_all(sent, ROWS, 0, 0, tiled=True)
        return jnp.sum(came.astype(jnp.float32), axis=0).reshape(-1, sent.shape[-1])

    def by_row(block):
        width = block.shape[1]
        parts = block.reshape(n_rows // 2, runs, 2, per, width)
        return parts.transpose(2, 0, 1, 3, 4).reshape(n_rows, runs * per, width)

    def by_z(block):
        width = block.shape[-1]
        parts = block.reshape(2, n_z, per, width)
        return jnp.swapaxes(parts, 0, 1).reshape(-1, width)

    def gather_z(pair):
        return lax.all_gather(pair.reshape(-1, features), "z", axis=0, tiled=True)

    def gather_rows(block):
        copies = lax.optimization_barrier(
            jnp.broadcast_to(block[None], (n_rows,) + block.shape)
        )
        every = lax.all_to_all(copies, ROWS, 0, 0, tiled=True)
        return every.reshape(n_rows, 2, -1, block.shape[1])

    both = lax.all_gather(outgoing(grad_out, stream_code, stream_scale), "yh", axis=0)
    stream_all = lax.all_gather(both[:, 1], ("z", "c"), axis=0)

    def first_half(both):
        grad_own = gather_z(both[:, 0])
        grad_other = swap(grad_own, "c")
        sent = blocks_of(
            dot_nt(grad_own, down_weight).astype(jnp.bfloat16),
            dot_nt(grad_other, down_weight).astype(jnp.bfloat16),
        )
        grad_act = scatter_rows(sent)
        positive = jnp.maximum(
            own_first(restore(hidden_code, hidden_scale)).astype(jnp.float32), 0.0
        )
        act = (positive * positive).astype(jnp.bfloat16)
        grad_pre = (grad_act * 2.0 * positive).astype(jnp.bfloat16)
        return grad_own, grad_other, gather_rows(grad_pre), act

    def skip(both):
        wide = jnp.zeros((n_z * 2 * per, features), jnp.bfloat16)
        pre = jnp.zeros((n_rows, 2, runs * per, hidden_width), jnp.bfloat16)
        return wide, wide, pre, jnp.zeros(hidden_code.shape, jnp.bfloat16)

    always = lax.optimization_barrier(jnp.bool_(True))
    grad_own, grad_other, grad_pre_all, act = lax.cond(always, first_half, skip, both)
    context = own_first(restore(ctx_code, ctx_scale))
    padding = jnp.zeros((act.shape[0], 512 - hidden_width - ctx_width), jnp.bfloat16)
    saved = jnp.concatenate([act, context, padding], axis=1)
    pre_own = by_z(grad_pre_all[:, 0])
    pre_other = by_z(grad_pre_all[:, 1])

    rows_own = grad_pre_all[:, 0].reshape(2, -1, hidden_width)
    came = swap(
        dot_nt(grad_pre_all[:, 1].reshape(-1, hidden_width), up_weight).astype(jnp.bfloat16), "c"
    ).reshape(2, -1, features)

    def stream_part(which):
        rows = lax.dynamic_index_in_dim(rows_own, which, 0, keepdims=False)
        other = lax.dynamic_index_in_dim(came, which, 0, keepdims=False)
        return dot_nt(rows, up_weight) + other.astype(jnp.float32)

    received = swap(stream_part(1 - half).astype(jnp.bfloat16), "yh")
    by_core = stream_all.reshape(n_z, 2, 2 * per, features)
    part = (stream_part(half) + received.astype(jnp.float32)).astype(jnp.bfloat16)
    part = part.reshape(n_z, per, features)
    part, saved, by_core = lax.optimization_barrier((part, saved, by_core))
    saved_all = lax.all_gather(saved, ROWS, axis=0)
    padded_out = jnp.pad(out_weight, ((0, -ctx_width % 128), (0, 0)))

    def second_half(part, by_core):
        came = lax.all_to_all(part, "z", 0, 0, tiled=True)
        stream_own = lax.dynamic_index_in_dim(by_core, core, 1, keepdims=False)
        stream_other = lax.dynamic_index_in_dim(by_core, 1 - core, 1, keepdims=False)
        stream_own = stream_own.reshape(-1, features)
        stream_other = stream_other.reshape(-1, features)
        grad_up = dot_tn(stream_own, pre_own) + dot_tn(stream_other, pre_other)
        came, grad_up = lax.optimization_barrier((came, grad_up))
        summed = jnp.sum(came.astype(jnp.float32), axis=0)
        grad_stream = (grad_out.astype(jnp.float32) + summed).astype(jnp.bfloat16)
        gs_own = gather_z(lax.all_gather(grad_stream, "yh", axis=0))
        gs_other = swap(gs_own, "c")
        sent = blocks_of(
            dot_nt(gs_own, padded_out).astype(jnp.bfloat16),
            dot_nt(gs_other, padded_out).astype(jnp.bfloat16),
        )
        return gs_own, gs_other, sent, grad_up

    def skip_second(part, by_core):
        wide = jnp.zeros((n_z * 2 * per, features), jnp.bfloat16)
        return (
            wide,
            wide,
            jnp.zeros((n_rows, 2, runs * per, padded_out.shape[0]), jnp.bfloat16),
            jnp.zeros((features, hidden_width), jnp.float32),
        )

    gs_own, gs_other, sent, grad_up = lax.cond(always, second_half, skip_second, part, by_core)
    sent, saved_all = lax.optimization_barrier((sent, saved_all))
    grad_ctx = natural(scatter_rows(sent)[:, :ctx_width].astype(jnp.bfloat16))
    grad_down, grad_outw = last_products(
        saved_all.reshape(n_rows, 2, -1, saved_all.shape[-1]),
        grad_own,
        grad_other,
        gs_own,
        gs_other,
        hidden_width,
        ctx_width,
    )
    return (grad_ctx, grad_outw, grad_up, grad_down)


def solution(mesh):
    parts = Mesh(mesh.devices.reshape(4, 2, 2, 16, 2), ROWS + COLS)
    by_cols, by_rows = P(COLS, ROWS), P(ROWS, COLS)
    in_specs = (
        by_cols,
        by_rows,
        by_rows,
        by_cols,
        by_cols,
        by_rows,
        by_rows,
        by_cols,
        by_rows,
        by_cols,
    )
    out_specs = (by_rows, by_cols, by_rows, by_cols)
    return jax.shard_map(local, mesh=parts, in_specs=in_specs, out_specs=out_specs, check_vma=False)
```

```python
import jax
import jax.numpy as jnp
from jax import lax
from jax.experimental import pallas as pl
from jax.experimental.pallas import tpu as pltpu
from jax.sharding import Mesh
from jax.sharding import PartitionSpec as P

QBLOCK = 32
PER = 16
ROWS = ("x", "yl")
COLS = ("yh", "z", "c")
SWAP = ((0, 1), (1, 0))


def restore(code, scale):
    count, width = code.shape
    blocks = code.astype(jnp.float32).reshape(count, width // QBLOCK, QBLOCK) * scale[:, :, None]
    return blocks.reshape(count, width).astype(jnp.bfloat16)


def dot_nt(left, right):
    return lax.dot_general(
        left, right, (((1,), (1,)), ((), ())), preferred_element_type=jnp.float32
    )


def dot_tn(left, right):
    return lax.dot_general(
        left, right, (((0,), (0,)), ((), ())), preferred_element_type=jnp.float32
    )


def outgoing_kernel(grad_ref, code_ref, scale_ref, out_ref):
    blocks, width = scale_ref.shape[1], code_ref.shape[1]
    row = lax.broadcasted_iota(jnp.int32, (blocks, width), 0)
    column = lax.broadcasted_iota(jnp.int32, (blocks, width), 1)
    first = row * QBLOCK
    spread = jnp.where((column >= first) & (column < first + QBLOCK), 1.0, 0.0)
    scale = jnp.dot(
        scale_ref[...],
        spread.astype(jnp.float32),
        precision=lax.Precision.HIGHEST,
        preferred_element_type=jnp.float32,
    )
    out_ref[0] = grad_ref[...]
    out_ref[1] = (code_ref[...].astype(jnp.float32) * scale).astype(jnp.bfloat16)


def outgoing(grad_out, code, scale):
    return pl.pallas_call(
        outgoing_kernel,
        out_shape=jax.ShapeDtypeStruct((2,) + grad_out.shape, jnp.bfloat16),
        in_specs=[pl.BlockSpec(memory_space=pltpu.VMEM)] * 3,
        out_specs=pl.BlockSpec(memory_space=pltpu.VMEM),
    )(grad_out, code, scale)


def row_blocks_kernel(own_ref, other_ref, weight_ref, out_ref):
    n_rows, _, block, _ = out_ref.shape
    runs = block // PER
    for side, ref in ((0, own_ref), (1, other_ref)):
        product = dot_nt(ref[...], weight_ref[...]).astype(jnp.bfloat16)
        for piece in range(n_rows * runs):
            layer, half = piece // 2, piece % 2
            row, run = half * (n_rows // 2) + layer // runs, layer % runs
            out_ref[row, side, pl.ds(run * PER, PER), :] = product[piece * PER : piece * PER + PER]


def row_blocks(own, other, weight, n_rows):
    width = weight.shape[0]
    return pl.pallas_call(
        row_blocks_kernel,
        out_shape=jax.ShapeDtypeStruct((n_rows, 2, own.shape[0] // n_rows, width), jnp.bfloat16),
        in_specs=[pl.BlockSpec(memory_space=pltpu.VMEM)] * 3,
        out_specs=pl.BlockSpec(memory_space=pltpu.VMEM),
        compiler_params=pltpu.CompilerParams(vmem_limit_bytes=32 * 2**20),
        cost_estimate=pl.CostEstimate(
            flops=4 * own.size * width, bytes_accessed=4 * own.size, transcendentals=0
        ),
    )(own, other, weight)


def last_kernel(
    saved_ref, grad_own_ref, grad_other_ref, gs_own_ref, gs_other_ref, down_ref, out_ref, rows_ref
):
    n_rows, _, block, wide = saved_ref.shape
    runs, per = rows_ref.shape[0] * 2 // n_rows, rows_ref.shape[2]
    hidden_width, ctx_width = down_ref.shape[0], out_ref.shape[0]
    for side, grad_ref, gs_ref in (
        (0, grad_own_ref, gs_own_ref),
        (1, grad_other_ref, gs_other_ref),
    ):
        for row in range(n_rows):
            half, first = row // (n_rows // 2), row % (n_rows // 2) * runs
            for run in range(runs):
                rows_ref[first + run, half] = saved_ref[row, side, pl.ds(run * per, per), :]
        rows = rows_ref[...].reshape(-1, wide)
        down = dot_tn(rows[:, :hidden_width], grad_ref[...])
        out = dot_tn(rows[:, hidden_width:], gs_ref[...])[:ctx_width]
        if side == 0:
            down_ref[...] = down
            out_ref[...] = out
        else:
            down_ref[...] += down
            out_ref[...] += out


def last_products(saved_all, grad_own, grad_other, gs_own, gs_other, hidden_width, ctx_width):
    features = grad_own.shape[1]
    return pl.pallas_call(
        last_kernel,
        out_shape=(
            jax.ShapeDtypeStruct((hidden_width, features), jnp.float32),
            jax.ShapeDtypeStruct((ctx_width, features), jnp.float32),
        ),
        in_specs=[pl.BlockSpec(memory_space=pltpu.VMEM)] * 5,
        out_specs=(pl.BlockSpec(memory_space=pltpu.VMEM),) * 2,
        scratch_shapes=[
            pltpu.VMEM((grad_own.shape[0] // (2 * PER), 2, PER, saved_all.shape[3]), jnp.bfloat16)
        ],
        compiler_params=pltpu.CompilerParams(vmem_limit_bytes=32 * 2**20),
        cost_estimate=pl.CostEstimate(
            flops=4 * grad_own.size * saved_all.shape[3],
            bytes_accessed=8 * grad_own.size + 2 * saved_all.size,
            transcendentals=0,
        ),
    )(saved_all, grad_own, grad_other, gs_own, gs_other)


def local(
    grad_out,
    ctx_code,
    ctx_scale,
    stream_code,
    stream_scale,
    hidden_code,
    hidden_scale,
    out_weight,
    up_weight,
    down_weight,
):
    core = lax.axis_index("c")
    half = lax.axis_index("yh")
    n_rows, n_z = lax.axis_size(ROWS), lax.axis_size("z")
    per = grad_out.shape[0]
    runs = n_z * 2 // n_rows
    features = grad_out.shape[1]
    hidden_width, ctx_width = hidden_code.shape[1], ctx_code.shape[1]

    def own_first(block):
        width = block.shape[1]
        parts = block.reshape(runs, 2, per, width)
        one, two = parts[:, 0], parts[:, 1]
        first = jnp.where(core == 0, one, two)
        second = jnp.where(core == 0, two, one)
        return jnp.stack([first, second]).reshape(block.shape)

    def natural(block):
        width = block.shape[1]
        parts = block.reshape(2, runs, per, width)
        one = jnp.where(core == 0, parts[0], parts[1])
        two = jnp.where(core == 0, parts[1], parts[0])
        return jnp.stack([one, two], axis=1).reshape(block.shape)

    def swap(block, axis):
        return lax.ppermute(block, axis, SWAP)

    def scatter_rows(sent):
        came = lax.all_to_all(sent, ROWS, 0, 0, tiled=True)
        return jnp.sum(came.astype(jnp.float32), axis=0).reshape(-1, sent.shape[-1])

    def by_z(block):
        width = block.shape[-1]
        parts = block.reshape(2, n_z, per, width)
        return jnp.swapaxes(parts, 0, 1).reshape(-1, width)

    def gather_z(pair):
        return lax.all_gather(pair.reshape(-1, features), "z", axis=0, tiled=True)

    def gather_rows(block):
        copies = lax.optimization_barrier(
            jnp.broadcast_to(block[None], (n_rows,) + block.shape)
        )
        every = lax.all_to_all(copies, ROWS, 0, 0, tiled=True)
        return every.reshape(n_rows, 2, -1, block.shape[1])

    both = lax.all_gather(outgoing(grad_out, stream_code, stream_scale), "yh", axis=0)
    stream_all = lax.all_gather(both[:, 1], ("z", "c"), axis=0)

    def first_half(both):
        grad_own = gather_z(both[:, 0])
        grad_other = swap(grad_own, "c")
        sent = row_blocks(grad_own, grad_other, down_weight, n_rows)
        grad_act = scatter_rows(sent)
        positive = jnp.maximum(
            own_first(restore(hidden_code, hidden_scale)).astype(jnp.float32), 0.0
        )
        act = (positive * positive).astype(jnp.bfloat16)
        grad_pre = (grad_act * 2.0 * positive).astype(jnp.bfloat16)
        return grad_own, grad_other, gather_rows(grad_pre), act

    def skip(both):
        wide = jnp.zeros((n_z * 2 * per, features), jnp.bfloat16)
        pre = jnp.zeros((n_rows, 2, runs * per, hidden_width), jnp.bfloat16)
        return wide, wide, pre, jnp.zeros(hidden_code.shape, jnp.bfloat16)

    always = lax.optimization_barrier(jnp.bool_(True))
    grad_own, grad_other, grad_pre_all, act = lax.cond(always, first_half, skip, both)
    context = own_first(restore(ctx_code, ctx_scale))
    padding = jnp.zeros((act.shape[0], 512 - hidden_width - ctx_width), jnp.bfloat16)
    saved = jnp.concatenate([act, context, padding], axis=1)
    pre_own = by_z(grad_pre_all[:, 0])
    pre_other = by_z(grad_pre_all[:, 1])

    came = swap(dot_nt(pre_other, up_weight).astype(jnp.bfloat16), "c")
    part = (dot_nt(pre_own, up_weight) + came.astype(jnp.float32)).reshape(n_z, 2, per, features)
    keep = lax.dynamic_index_in_dim(part, half, 1, keepdims=False)
    send = lax.dynamic_index_in_dim(part, 1 - half, 1, keepdims=False).astype(jnp.bfloat16)
    received = swap(send, "yh")
    by_core = stream_all.reshape(n_z, 2, 2 * per, features)
    received, saved, by_core = lax.optimization_barrier((received, saved, by_core))
    saved_all = lax.all_gather(saved, ROWS, axis=0)
    padded_out = jnp.pad(out_weight, ((0, -ctx_width % 128), (0, 0)))

    def second_half(keep, received, by_core):
        part = (keep + received.astype(jnp.float32)).astype(jnp.bfloat16)
        came = lax.all_to_all(part, "z", 0, 0, tiled=True)
        stream_own = lax.dynamic_index_in_dim(by_core, core, 1, keepdims=False)
        stream_other = lax.dynamic_index_in_dim(by_core, 1 - core, 1, keepdims=False)
        stream_own = stream_own.reshape(-1, features)
        stream_other = stream_other.reshape(-1, features)
        grad_up = dot_tn(stream_own, pre_own) + dot_tn(stream_other, pre_other)
        came, grad_up = lax.optimization_barrier((came, grad_up))
        summed = jnp.sum(came.astype(jnp.float32), axis=0)
        grad_stream = (grad_out.astype(jnp.float32) + summed).astype(jnp.bfloat16)
        gs_own = gather_z(lax.all_gather(grad_stream, "yh", axis=0))
        gs_other = swap(gs_own, "c")
        sent = row_blocks(gs_own, gs_other, padded_out, n_rows)
        return gs_own, gs_other, sent, grad_up

    def skip_second(keep, received, by_core):
        wide = jnp.zeros((n_z * 2 * per, features), jnp.bfloat16)
        return (
            wide,
            wide,
            jnp.zeros((n_rows, 2, runs * per, padded_out.shape[0]), jnp.bfloat16),
            jnp.zeros((features, hidden_width), jnp.float32),
        )

    gs_own, gs_other, sent, grad_up = lax.cond(
        always, second_half, skip_second, keep, received, by_core
    )
    sent, saved_all = lax.optimization_barrier((sent, saved_all))
    grad_ctx = natural(scatter_rows(sent)[:, :ctx_width].astype(jnp.bfloat16))
    grad_down, grad_outw = last_products(
        saved_all.reshape(n_rows, 2, -1, saved_all.shape[-1]),
        grad_own,
        grad_other,
        gs_own,
        gs_other,
        hidden_width,
        ctx_width,
    )
    return (grad_ctx, grad_outw, grad_up, grad_down)


def solution(mesh):
    parts = Mesh(mesh.devices.reshape(4, 2, 2, 16, 2), ROWS + COLS)
    by_cols, by_rows = P(COLS, ROWS), P(ROWS, COLS)
    in_specs = (
        by_cols,
        by_rows,
        by_rows,
        by_cols,
        by_cols,
        by_rows,
        by_rows,
        by_cols,
        by_rows,
        by_cols,
    )
    out_specs = (by_rows, by_cols, by_rows, by_cols)
    return jax.shard_map(local, mesh=parts, in_specs=in_specs, out_specs=out_specs, check_vma=False)
```

```python
import jax
import jax.numpy as jnp
from jax import lax
from jax.experimental import pallas as pl
from jax.experimental.pallas import tpu as pltpu
from jax.sharding import Mesh
from jax.sharding import PartitionSpec as P

QBLOCK = 32
PER = 16
ROWS = ("x", "yl")
COLS = ("yh", "z", "c")
SWAP = ((0, 1), (1, 0))


def restore(code, scale):
    count, width = code.shape
    blocks = code.astype(jnp.float32).reshape(count, width // QBLOCK, QBLOCK) * scale[:, :, None]
    return blocks.reshape(count, width).astype(jnp.bfloat16)


def dot_nt(left, right):
    return lax.dot_general(
        left, right, (((1,), (1,)), ((), ())), preferred_element_type=jnp.float32
    )


def dot_tn(left, right):
    return lax.dot_general(
        left, right, (((0,), (0,)), ((), ())), preferred_element_type=jnp.float32
    )


def outgoing_kernel(grad_ref, code_ref, scale_ref, out_ref):
    blocks, width = scale_ref.shape[1], code_ref.shape[1]
    row = lax.broadcasted_iota(jnp.int32, (blocks, width), 0)
    column = lax.broadcasted_iota(jnp.int32, (blocks, width), 1)
    first = row * QBLOCK
    spread = jnp.where((column >= first) & (column < first + QBLOCK), 1.0, 0.0)
    scale = jnp.dot(
        scale_ref[...],
        spread.astype(jnp.float32),
        precision=lax.Precision.HIGHEST,
        preferred_element_type=jnp.float32,
    )
    out_ref[0] = grad_ref[...]
    out_ref[1] = (code_ref[...].astype(jnp.float32) * scale).astype(jnp.bfloat16)


def outgoing(grad_out, code, scale):
    return pl.pallas_call(
        outgoing_kernel,
        out_shape=jax.ShapeDtypeStruct((2,) + grad_out.shape, jnp.bfloat16),
        in_specs=[pl.BlockSpec(memory_space=pltpu.VMEM)] * 3,
        out_specs=pl.BlockSpec(memory_space=pltpu.VMEM),
    )(grad_out, code, scale)


def last_kernel(
    saved_ref, grad_own_ref, grad_other_ref, gs_own_ref, gs_other_ref, down_ref, out_ref, rows_ref
):
    n_rows, _, block, wide = saved_ref.shape
    runs, per = rows_ref.shape[0] * 2 // n_rows, rows_ref.shape[2]
    hidden_width, ctx_width = down_ref.shape[0], out_ref.shape[0]
    for side, grad_ref, gs_ref in (
        (0, grad_own_ref, gs_own_ref),
        (1, grad_other_ref, gs_other_ref),
    ):
        for row in range(n_rows):
            half, first = row // (n_rows // 2), row % (n_rows // 2) * runs
            for run in range(runs):
                rows_ref[first + run, half] = saved_ref[row, side, pl.ds(run * per, per), :]
        rows = rows_ref[...].reshape(-1, wide)
        down = dot_tn(rows[:, :hidden_width], grad_ref[...])
        out = dot_tn(rows[:, hidden_width:], gs_ref[...])[:ctx_width]
        if side == 0:
            down_ref[...] = down
            out_ref[...] = out
        else:
            down_ref[...] += down
            out_ref[...] += out


def last_products(saved_all, grad_own, grad_other, gs_own, gs_other, hidden_width, ctx_width):
    features = grad_own.shape[1]
    return pl.pallas_call(
        last_kernel,
        out_shape=(
            jax.ShapeDtypeStruct((hidden_width, features), jnp.float32),
            jax.ShapeDtypeStruct((ctx_width, features), jnp.float32),
        ),
        in_specs=[pl.BlockSpec(memory_space=pltpu.VMEM)] * 5,
        out_specs=(pl.BlockSpec(memory_space=pltpu.VMEM),) * 2,
        scratch_shapes=[
            pltpu.VMEM((grad_own.shape[0] // (2 * PER), 2, PER, saved_all.shape[3]), jnp.bfloat16)
        ],
        compiler_params=pltpu.CompilerParams(vmem_limit_bytes=32 * 2**20),
        cost_estimate=pl.CostEstimate(
            flops=4 * grad_own.size * saved_all.shape[3],
            bytes_accessed=8 * grad_own.size + 2 * saved_all.size,
            transcendentals=0,
        ),
    )(saved_all, grad_own, grad_other, gs_own, gs_other)


def local(
    grad_out,
    ctx_code,
    ctx_scale,
    stream_code,
    stream_scale,
    hidden_code,
    hidden_scale,
    out_weight,
    up_weight,
    down_weight,
):
    core = lax.axis_index("c")
    half = lax.axis_index("yh")
    n_rows, n_z = lax.axis_size(ROWS), lax.axis_size("z")
    per = grad_out.shape[0]
    runs = n_z * 2 // n_rows
    features = grad_out.shape[1]
    hidden_width, ctx_width = hidden_code.shape[1], ctx_code.shape[1]

    def own_first(block):
        width = block.shape[1]
        parts = block.reshape(runs, 2, per, width)
        one, two = parts[:, 0], parts[:, 1]
        first = jnp.where(core == 0, one, two)
        second = jnp.where(core == 0, two, one)
        return jnp.stack([first, second]).reshape(block.shape)

    def natural(block):
        width = block.shape[1]
        parts = block.reshape(2, runs, per, width)
        one = jnp.where(core == 0, parts[0], parts[1])
        two = jnp.where(core == 0, parts[1], parts[0])
        return jnp.stack([one, two], axis=1).reshape(block.shape)

    def swap(block, axis):
        return lax.ppermute(block, axis, SWAP)

    def blocks_of(own, other):
        return jnp.stack([by_row(own), by_row(other)], axis=1)

    def scatter_rows(sent):
        came = lax.all_to_all(sent, ROWS, 0, 0, tiled=True)
        return jnp.sum(came.astype(jnp.float32), axis=0).reshape(-1, sent.shape[-1])

    def by_row(block):
        width = block.shape[1]
        parts = block.reshape(n_rows // 2, runs, 2, per, width)
        return parts.transpose(2, 0, 1, 3, 4).reshape(n_rows, runs * per, width)

    def by_z(block):
        width = block.shape[-1]
        parts = block.reshape(2, n_z, per, width)
        return jnp.swapaxes(parts, 0, 1).reshape(-1, width)

    def gather_z(pair):
        return lax.all_gather(pair.reshape(-1, features), "z", axis=0, tiled=True)

    def gather_rows(block):
        copies = lax.optimization_barrier(
            jnp.broadcast_to(block[None], (n_rows,) + block.shape)
        )
        every = lax.all_to_all(copies, ROWS, 0, 0, tiled=True)
        return every.reshape(n_rows, 2, -1, block.shape[1])

    both = lax.all_gather(outgoing(grad_out, stream_code, stream_scale), "yh", axis=0)
    stream_all = lax.all_gather(both[:, 1], ("z", "c"), axis=0)

    def first_half(both):
        grad_own = gather_z(both[:, 0])
        grad_other = swap(grad_own, "c")
        sent = blocks_of(
            dot_nt(grad_own, down_weight).astype(jnp.bfloat16),
            dot_nt(grad_other, down_weight).astype(jnp.bfloat16),
        )
        grad_act = scatter_rows(sent)
        positive = jnp.maximum(
            own_first(restore(hidden_code, hidden_scale)).astype(jnp.float32), 0.0
        )
        act = (positive * positive).astype(jnp.bfloat16)
        grad_pre = (grad_act * 2.0 * positive).astype(jnp.bfloat16)
        return grad_own, grad_other, gather_rows(grad_pre), act

    def skip(both):
        wide = jnp.zeros((n_z * 2 * per, features), jnp.bfloat16)
        pre = jnp.zeros((n_rows, 2, runs * per, hidden_width), jnp.bfloat16)
        return wide, wide, pre, jnp.zeros(hidden_code.shape, jnp.bfloat16)

    always = lax.optimization_barrier(jnp.bool_(True))
    grad_own, grad_other, grad_pre_all, act = lax.cond(always, first_half, skip, both)
    context = own_first(restore(ctx_code, ctx_scale))
    padding = jnp.zeros((act.shape[0], 512 - hidden_width - ctx_width), jnp.bfloat16)
    saved = jnp.concatenate([act, context, padding], axis=1)
    pre_own = by_z(grad_pre_all[:, 0])
    pre_other = by_z(grad_pre_all[:, 1])

    came = swap(dot_nt(pre_other, up_weight).astype(jnp.bfloat16), "c")
    part = (dot_nt(pre_own, up_weight) + came.astype(jnp.float32)).reshape(n_z, 2, per, features)
    keep = lax.dynamic_index_in_dim(part, half, 1, keepdims=False)
    send = lax.dynamic_index_in_dim(part, 1 - half, 1, keepdims=False).astype(jnp.bfloat16)
    by_core = stream_all.reshape(n_z, 2, 2 * per, features)
    send, saved, by_core = lax.optimization_barrier((send, saved, by_core))
    saved_all = lax.all_gather(saved, ROWS, axis=0)
    padded_out = jnp.pad(out_weight, ((0, -ctx_width % 128), (0, 0)))

    def second_half(keep, send, by_core):
        part = (keep + swap(send, "yh").astype(jnp.float32)).astype(jnp.bfloat16)
        came = lax.all_to_all(part, "z", 0, 0, tiled=True)
        stream_own = lax.dynamic_index_in_dim(by_core, core, 1, keepdims=False)
        stream_other = lax.dynamic_index_in_dim(by_core, 1 - core, 1, keepdims=False)
        stream_own = stream_own.reshape(-1, features)
        stream_other = stream_other.reshape(-1, features)
        grad_up = dot_tn(stream_own, pre_own) + dot_tn(stream_other, pre_other)
        came, grad_up = lax.optimization_barrier((came, grad_up))
        summed = jnp.sum(came.astype(jnp.float32), axis=0)
        grad_stream = (grad_out.astype(jnp.float32) + summed).astype(jnp.bfloat16)
        gs_own = gather_z(lax.all_gather(grad_stream, "yh", axis=0))
        gs_other = swap(gs_own, "c")
        sent = blocks_of(
            dot_nt(gs_own, padded_out).astype(jnp.bfloat16),
            dot_nt(gs_other, padded_out).astype(jnp.bfloat16),
        )
        return gs_own, gs_other, sent, grad_up

    def skip_second(keep, send, by_core):
        wide = jnp.zeros((n_z * 2 * per, features), jnp.bfloat16)
        return (
            wide,
            wide,
            jnp.zeros((n_rows, 2, runs * per, padded_out.shape[0]), jnp.bfloat16),
            jnp.zeros((features, hidden_width), jnp.float32),
        )

    gs_own, gs_other, sent, grad_up = lax.cond(
        always, second_half, skip_second, keep, send, by_core
    )
    sent, saved_all = lax.optimization_barrier((sent, saved_all))
    grad_ctx = natural(scatter_rows(sent)[:, :ctx_width].astype(jnp.bfloat16))
    grad_down, grad_outw = last_products(
        saved_all.reshape(n_rows, 2, -1, saved_all.shape[-1]),
        grad_own,
        grad_other,
        gs_own,
        gs_other,
        hidden_width,
        ctx_width,
    )
    return (grad_ctx, grad_outw, grad_up, grad_down)


def solution(mesh):
    parts = Mesh(mesh.devices.reshape(4, 2, 2, 16, 2), ROWS + COLS)
    by_cols, by_rows = P(COLS, ROWS), P(ROWS, COLS)
    in_specs = (
        by_cols,
        by_rows,
        by_rows,
        by_cols,
        by_cols,
        by_rows,
        by_rows,
        by_cols,
        by_rows,
        by_cols,
    )
    out_specs = (by_rows, by_cols, by_rows, by_cols)
    return jax.shard_map(local, mesh=parts, in_specs=in_specs, out_specs=out_specs, check_vma=False)
```

```python
import jax
import jax.numpy as jnp
from jax import lax
from jax.experimental import pallas as pl
from jax.experimental.pallas import tpu as pltpu
from jax.sharding import Mesh
from jax.sharding import PartitionSpec as P

QBLOCK = 32
PER = 16
ROWS = ("x", "yl")
COLS = ("yh", "z", "c")
SWAP = ((0, 1), (1, 0))


def restore(code, scale):
    count, width = code.shape
    blocks = code.astype(jnp.float32).reshape(count, width // QBLOCK, QBLOCK) * scale[:, :, None]
    return blocks.reshape(count, width).astype(jnp.bfloat16)


def dot_nt(left, right):
    return lax.dot_general(
        left, right, (((1,), (1,)), ((), ())), preferred_element_type=jnp.float32
    )


def dot_tn(left, right):
    return lax.dot_general(
        left, right, (((0,), (0,)), ((), ())), preferred_element_type=jnp.float32
    )


def outgoing_kernel(grad_ref, code_ref, scale_ref, out_ref):
    blocks, width = scale_ref.shape[1], code_ref.shape[1]
    row = lax.broadcasted_iota(jnp.int32, (blocks, width), 0)
    column = lax.broadcasted_iota(jnp.int32, (blocks, width), 1)
    first = row * QBLOCK
    spread = jnp.where((column >= first) & (column < first + QBLOCK), 1.0, 0.0)
    scale = jnp.dot(
        scale_ref[...],
        spread.astype(jnp.float32),
        precision=lax.Precision.HIGHEST,
        preferred_element_type=jnp.float32,
    )
    out_ref[0] = grad_ref[...]
    out_ref[1] = (code_ref[...].astype(jnp.float32) * scale).astype(jnp.bfloat16)


def outgoing(grad_out, code, scale):
    return pl.pallas_call(
        outgoing_kernel,
        out_shape=jax.ShapeDtypeStruct((2,) + grad_out.shape, jnp.bfloat16),
        in_specs=[pl.BlockSpec(memory_space=pltpu.VMEM)] * 3,
        out_specs=pl.BlockSpec(memory_space=pltpu.VMEM),
    )(grad_out, code, scale)


def last_kernel(
    saved_ref, grad_own_ref, grad_other_ref, gs_own_ref, gs_other_ref, down_ref, out_ref, rows_ref
):
    n_rows, _, block, wide = saved_ref.shape
    runs, per = rows_ref.shape[0] * 2 // n_rows, rows_ref.shape[2]
    hidden_width, ctx_width = down_ref.shape[0], out_ref.shape[0]
    for side, grad_ref, gs_ref in (
        (0, grad_own_ref, gs_own_ref),
        (1, grad_other_ref, gs_other_ref),
    ):
        for row in range(n_rows):
            half, first = row // (n_rows // 2), row % (n_rows // 2) * runs
            for run in range(runs):
                rows_ref[first + run, half] = saved_ref[row, side, pl.ds(run * per, per), :]
        rows = rows_ref[...].reshape(-1, wide)
        down = dot_tn(rows[:, :hidden_width], grad_ref[...])
        out = dot_tn(rows[:, hidden_width:], gs_ref[...])[:ctx_width]
        if side == 0:
            down_ref[...] = down
            out_ref[...] = out
        else:
            down_ref[...] += down
            out_ref[...] += out


def last_products(saved_all, grad_own, grad_other, gs_own, gs_other, hidden_width, ctx_width):
    features = grad_own.shape[1]
    return pl.pallas_call(
        last_kernel,
        out_shape=(
            jax.ShapeDtypeStruct((hidden_width, features), jnp.float32),
            jax.ShapeDtypeStruct((ctx_width, features), jnp.float32),
        ),
        in_specs=[pl.BlockSpec(memory_space=pltpu.VMEM)] * 5,
        out_specs=(pl.BlockSpec(memory_space=pltpu.VMEM),) * 2,
        scratch_shapes=[
            pltpu.VMEM((grad_own.shape[0] // (2 * PER), 2, PER, saved_all.shape[3]), jnp.bfloat16)
        ],
        compiler_params=pltpu.CompilerParams(vmem_limit_bytes=32 * 2**20),
        cost_estimate=pl.CostEstimate(
            flops=4 * grad_own.size * saved_all.shape[3],
            bytes_accessed=8 * grad_own.size + 2 * saved_all.size,
            transcendentals=0,
        ),
    )(saved_all, grad_own, grad_other, gs_own, gs_other)


def local(
    grad_out,
    ctx_code,
    ctx_scale,
    stream_code,
    stream_scale,
    hidden_code,
    hidden_scale,
    out_weight,
    up_weight,
    down_weight,
):
    core = lax.axis_index("c")
    half = lax.axis_index("yh")
    n_rows, n_z = lax.axis_size(ROWS), lax.axis_size("z")
    per = grad_out.shape[0]
    runs = n_z * 2 // n_rows
    features = grad_out.shape[1]
    hidden_width, ctx_width = hidden_code.shape[1], ctx_code.shape[1]

    def own_first(block):
        width = block.shape[1]
        parts = block.reshape(runs, 2, per, width)
        one, two = parts[:, 0], parts[:, 1]
        first = jnp.where(core == 0, one, two)
        second = jnp.where(core == 0, two, one)
        return jnp.stack([first, second]).reshape(block.shape)

    def natural(block):
        width = block.shape[1]
        parts = block.reshape(2, runs, per, width)
        one = jnp.where(core == 0, parts[0], parts[1])
        two = jnp.where(core == 0, parts[1], parts[0])
        return jnp.stack([one, two], axis=1).reshape(block.shape)

    def swap(block, axis):
        return lax.ppermute(block, axis, SWAP)

    def blocks_of(own, other):
        return jnp.stack([by_row(own), by_row(other)], axis=1)

    def scatter_rows(sent):
        came = lax.all_to_all(sent, ROWS, 0, 0, tiled=True)
        return jnp.sum(came.astype(jnp.float32), axis=0).reshape(-1, sent.shape[-1])

    def by_row(block):
        width = block.shape[1]
        parts = block.reshape(n_rows // 2, runs, 2, per, width)
        return parts.transpose(2, 0, 1, 3, 4).reshape(n_rows, runs * per, width)

    def by_z(block):
        width = block.shape[-1]
        parts = block.reshape(2, n_z, per, width)
        return jnp.swapaxes(parts, 0, 1).reshape(-1, width)

    def gather_z(pair):
        return lax.all_gather(pair.reshape(-1, features), "z", axis=0, tiled=True)

    def gather_rows(block):
        copies = lax.optimization_barrier(
            jnp.broadcast_to(block[None], (n_rows,) + block.shape)
        )
        every = lax.all_to_all(copies, ROWS, 0, 0, tiled=True)
        return every.reshape(n_rows, 2, -1, block.shape[1])

    both = lax.all_gather(outgoing(grad_out, stream_code, stream_scale), "yh", axis=0)
    stream_all = lax.all_gather(both[:, 1], ("z", "c"), axis=0)

    def first_half(both):
        grad_own = gather_z(both[:, 0])
        grad_other = swap(grad_own, "c")
        sent = blocks_of(
            dot_nt(grad_own, down_weight).astype(jnp.bfloat16),
            dot_nt(grad_other, down_weight).astype(jnp.bfloat16),
        )
        grad_act = scatter_rows(sent)
        positive = jnp.maximum(
            own_first(restore(hidden_code, hidden_scale)).astype(jnp.float32), 0.0
        )
        act = (positive * positive).astype(jnp.bfloat16)
        grad_pre = (grad_act * 2.0 * positive).astype(jnp.bfloat16)
        return grad_own, grad_other, gather_rows(grad_pre), act

    def skip(both):
        wide = jnp.zeros((n_z * 2 * per, features), jnp.bfloat16)
        pre = jnp.zeros((n_rows, 2, runs * per, hidden_width), jnp.bfloat16)
        return wide, wide, pre, jnp.zeros(hidden_code.shape, jnp.bfloat16)

    always = lax.optimization_barrier(jnp.bool_(True))
    grad_own, grad_other, grad_pre_all, act = lax.cond(always, first_half, skip, both)
    context = own_first(restore(ctx_code, ctx_scale))
    padding = jnp.zeros((act.shape[0], 512 - hidden_width - ctx_width), jnp.bfloat16)
    saved = jnp.concatenate([act, context, padding], axis=1)
    pre_own = by_z(grad_pre_all[:, 0])
    pre_other = by_z(grad_pre_all[:, 1])

    came = swap(dot_nt(pre_other, up_weight).astype(jnp.bfloat16), "c")
    part = (dot_nt(pre_own, up_weight) + came.astype(jnp.float32)).reshape(n_z, 2, per, features)
    keep = lax.dynamic_index_in_dim(part, half, 1, keepdims=False)
    send = lax.dynamic_index_in_dim(part, 1 - half, 1, keepdims=False).astype(jnp.bfloat16)
    by_core = stream_all.reshape(n_z, 2, 2 * per, features)
    send, saved, by_core = lax.optimization_barrier((send, saved, by_core))
    saved_all = lax.all_gather(saved, ROWS, axis=0)
    padded_width = ctx_width + -ctx_width % 128

    def second_half(keep, send, by_core):
        part = (keep + swap(send, "yh").astype(jnp.float32)).astype(jnp.bfloat16)
        came = lax.all_to_all(part, "z", 0, 0, tiled=True)
        padded_out = jnp.pad(out_weight, ((0, padded_width - ctx_width), (0, 0)))
        stream_own = lax.dynamic_index_in_dim(by_core, core, 1, keepdims=False)
        stream_other = lax.dynamic_index_in_dim(by_core, 1 - core, 1, keepdims=False)
        stream_own = stream_own.reshape(-1, features)
        stream_other = stream_other.reshape(-1, features)
        grad_up = dot_tn(stream_own, pre_own) + dot_tn(stream_other, pre_other)
        came, grad_up, padded_out = lax.optimization_barrier((came, grad_up, padded_out))
        summed = jnp.sum(came.astype(jnp.float32), axis=0)
        grad_stream = (grad_out.astype(jnp.float32) + summed).astype(jnp.bfloat16)
        gs_own = gather_z(lax.all_gather(grad_stream, "yh", axis=0))
        gs_other = swap(gs_own, "c")
        sent = blocks_of(
            dot_nt(gs_own, padded_out).astype(jnp.bfloat16),
            dot_nt(gs_other, padded_out).astype(jnp.bfloat16),
        )
        return gs_own, gs_other, sent, grad_up

    def skip_second(keep, send, by_core):
        wide = jnp.zeros((n_z * 2 * per, features), jnp.bfloat16)
        return (
            wide,
            wide,
            jnp.zeros((n_rows, 2, runs * per, padded_width), jnp.bfloat16),
            jnp.zeros((features, hidden_width), jnp.float32),
        )

    gs_own, gs_other, sent, grad_up = lax.cond(
        always, second_half, skip_second, keep, send, by_core
    )
    sent, saved_all = lax.optimization_barrier((sent, saved_all))
    grad_ctx = natural(scatter_rows(sent)[:, :ctx_width].astype(jnp.bfloat16))
    grad_down, grad_outw = last_products(
        saved_all.reshape(n_rows, 2, -1, saved_all.shape[-1]),
        grad_own,
        grad_other,
        gs_own,
        gs_other,
        hidden_width,
        ctx_width,
    )
    return (grad_ctx, grad_outw, grad_up, grad_down)


def solution(mesh):
    parts = Mesh(mesh.devices.reshape(4, 2, 2, 16, 2), ROWS + COLS)
    by_cols, by_rows = P(COLS, ROWS), P(ROWS, COLS)
    in_specs = (
        by_cols,
        by_rows,
        by_rows,
        by_cols,
        by_cols,
        by_rows,
        by_rows,
        by_cols,
        by_rows,
        by_cols,
    )
    out_specs = (by_rows, by_cols, by_rows, by_cols)
    return jax.shard_map(local, mesh=parts, in_specs=in_specs, out_specs=out_specs, check_vma=False)
```
